32 devices in a mesh: traj: 2 (over x), frame: 4 (over y, core), patch: 4 (over z).
Axes of the slice: x: 2, y: 2, z: 4, core: 2. Of those that a mesh axis runs over, the one named last changes fastest.
Arguments:
- queries: float32 [16, 256, 1024], P(('traj', 'frame'), 'patch'), parts along dimension 0, may hold values from -64 to 64
- key_rows: float32 [16, 256, 1024], P(('traj', 'frame'), 'patch'), parts along dimension 0, may hold values from -5 to 5
- value_rows: float32 [16, 256, 1024], P(('traj', 'frame'), 'patch'), parts along dimension 0, may hold values from -6 to 6
- cotangent: float32 [16, 256, 1024], P(('traj', 'frame'), 'patch'), parts along dimension 0, may hold values from -6 to 6
- lookback: int32 [16], P(('traj', 'frame')), parts along dimension 0, may hold values from 2 to 6
- window: int32 [32, 12], P(('traj', 'patch')), parts along dimension 0, may hold values from 0 to 15, as said below
Outputs:
- mixed: float32 [16, 256, 1024], P(('traj', 'frame'), 'patch'), parts along dimension 0
- grad_queries: float32 [16, 256, 1024], P(('traj', 'frame'), 'patch'), parts along dimension 0
- grad_keys: float32 [16, 256, 1024], P(('traj', 'frame'), 'patch'), parts along dimension 0
- grad_values: float32 [16, 256, 1024], P(('traj', 'frame'), 'patch'), parts along dimension 0
The draws below stay inside these ranges and needn't reach their ends.
There are 2 independent parts, one for each index of `traj`. The reference program is written for one: setup_inputs(seed, part) draws one part's arguments, and reference() takes and returns one part's arrays. A program takes and returns all parts, laid end to end along the dimension named above; each array names one. Nothing has to cross between parts.
Inputs may be any that keep to these rules, and one draw needn't show every extreme that they name: `window`: row b lists 12 distinct blocks: b itself first, then blocks at cyclic distance 1 to 6 from b among the 16 blocks.
All inputs are finite; a program needn't handle non-finite values.
Results may differ from the reference program's by a relative error of at most 0.0003.
Values sent between devices are 32-bit elements; how exact they have to be, the bound alone decides.
No kernel may reach another device: no remote copies, remote signals or barrier semaphores. Data moves between devices by JAX's collectives and lax.ppermute only.
A program may use at most 128 MiB of HBM per device.

```python
import math
from functools import partial
import jax
import jax.numpy as jnp
from jax import lax

H = 16
E = 64
BLK = 16
NW = 12
D = 1024
LOOK = 6
REACH = 6
F = 8
P_SIZE = 256


def draw_queries(key, part):
    key = jax.random.fold_in(key, 5)
    result = jnp.clip(jax.random.normal(key, (F, P_SIZE, H * E), jnp.float32), -5.0, 5.0)
    return result


def draw_key_rows(key, part):
    key = jax.random.fold_in(key, 6)
    result = jnp.clip(jax.random.normal(key, (F, P_SIZE, H * E), jnp.float32), -5.0, 5.0)
    return result


def draw_lookback(key, part):
    key = jax.random.fold_in(key, 7)
    drawn = jax.random.randint(key, (F,), 2, LOOK + 1)
    return drawn.at[F - 1].set(LOOK).astype(jnp.int32)


def draw_window(key, part):
    key = jax.random.fold_in(key, 9)
    block_count = P_SIZE // BLK
    option_count = 2 * REACH
    ranks = jax.random.randint(key, (block_count, option_count), 0, 1 << 20) * option_count + jnp.arange(option_count, dtype=jnp.int32)[None, :]
    ranking = jnp.argsort(ranks, axis=1)
    offsets_all = jnp.concatenate([jnp.arange(-REACH, 0, dtype=jnp.int32), jnp.arange(1, REACH + 1, dtype=jnp.int32)])
    chosen = offsets_all[ranking[:, :NW - 1]]
    blocks = jnp.arange(block_count, dtype=jnp.int32)[:, None]
    others = (blocks + chosen) % block_count
    return jnp.concatenate([blocks, others], axis=1).astype(jnp.int32)


def block_scale(rng, shape, shards, low, largest):
    level, own = 1.0, jax.random.fold_in(rng, 6)
    for axis_at, blocks in shards:
        steps = jnp.exp(jax.random.uniform(jax.random.fold_in(own, axis_at), (blocks,), jnp.float32, low / len(shards), largest / len(shards)))
        level = level * jnp.repeat(steps, shape[axis_at] // blocks).reshape([-1 if axis == axis_at else 1 for axis in range(len(shape))])
    return level


def centred(key, shape, scale, most, cuts=(), kind=jnp.bfloat16):
    level = block_scale(key, shape, cuts, -0.22, 0.18) if cuts else 1.0
    array = jax.random.normal(key, shape, jnp.float32) * scale * level
    return jnp.minimum(jnp.maximum(array, -most), most).astype(kind)


def setup_inputs(seed: int = 0, part: int = 0) -> dict:
    arg_keys = jax.random.split(jax.random.key(seed), 7)
    own_keys = jax.random.split(jax.random.fold_in(arg_keys[6], part), 7)
    return {
        "queries": draw_queries(jax.random.fold_in(jax.random.fold_in(arg_keys[6], part), 71), part),
        "key_rows": draw_key_rows(jax.random.fold_in(jax.random.fold_in(arg_keys[6], part), 71), part),
        "value_rows": centred(own_keys[2], (F, P_SIZE, D), 1.0, 6.0, ((0, 4), (1, 4)), jnp.float32),
        "cotangent": centred(own_keys[3], (F, P_SIZE, D), 1.0, 6.0, ((0, 4), (1, 4)), jnp.float32),
        "lookback": draw_lookback(jax.random.fold_in(jax.random.fold_in(arg_keys[6], part), 71), part),
        "window": draw_window(jax.random.fold_in(jax.random.fold_in(arg_keys[6], part), 71), part),
    }


def split_heads(tensor):
    return tensor.reshape(tensor.shape[0], tensor.shape[1], H, E)

def temporal_attention(queries, key_rows, value_rows, lookback):
    frame_ids = jnp.arange(F, dtype=jnp.int32)
    frame_gap = frame_ids[:, None] - frame_ids[None, :]
    visible = (frame_gap >= 0) & (frame_gap < lookback[:, None])
    scores = jnp.einsum('fphe,jphe->phfj', split_heads(queries), split_heads(key_rows), precision=lax.Precision.HIGHEST) * (1.0 / math.sqrt(E))
    scores = jnp.where(visible, scores, -jnp.inf)
    weights = jax.nn.softmax(scores, axis=-1)
    result = jnp.einsum('phfj,jphe->fphe', weights, split_heads(value_rows), precision=lax.Precision.HIGHEST)
    return result.reshape(F, P_SIZE, H * E)

def spatial_attention(queries, key_rows, value_rows, window):
    block_count = P_SIZE // BLK
    allowed_blocks = jnp.any(window[:, :, None] == jnp.arange(block_count, dtype=jnp.int32)[None, None, :], axis=1)
    block_of = jnp.arange(P_SIZE, dtype=jnp.int32) // BLK
    allowed = allowed_blocks[block_of][:, block_of]

    def per_frame(frame_items):
        query_frame, key_frame, value_frame = frame_items
        scores = jnp.einsum('phe,xhe->hpx', query_frame.reshape(P_SIZE, H, E), key_frame.reshape(P_SIZE, H, E), precision=lax.Precision.HIGHEST) * (1.0 / math.sqrt(E))
        scores = jnp.where(allowed[None], scores, -jnp.inf)
        weights = jax.nn.softmax(scores, axis=-1)
        result = jnp.einsum('hpx,xhe->phe', weights, value_frame.reshape(P_SIZE, H, E), precision=lax.Precision.HIGHEST)
        return result.reshape(P_SIZE, H * E)
    return lax.map(jax.checkpoint(per_frame), (queries, key_rows, value_rows))

def forward_pass(queries, key_rows, value_rows, lookback, window):
    temporal = temporal_attention(queries, key_rows, value_rows, lookback)
    return spatial_attention(queries, key_rows, temporal, window)

def reference(queries, key_rows, value_rows, cotangent, lookback, window):
    mixed, pullback = jax.vjp(partial(forward_pass, lookback=lookback, window=window), queries, key_rows, value_rows)
    gradients = pullback(cotangent)
    return (mixed, gradients[0], gradients[1], gradients[2])
```

```python
import math

import jax
import jax.numpy as jnp
from jax import lax
from jax.experimental import pallas as pl
from jax.experimental.pallas import tpu as pltpu
from jax.sharding import PartitionSpec as P

H = 16
BLK = 16
LOOK = 6
REACH = 6


def shifted(x, axis, by):
    count = lax.axis_size(axis)
    pairs = [(i, i + by) for i in range(count) if 0 <= i + by < count]
    return lax.ppermute(x, axis, pairs)


def passed_along(block, axis, distance):
    devices = range(lax.axis_size(axis))
    route = [((i - distance) % len(devices), i) for i in devices]
    return lax.ppermute(block, axis, route)


def split_heads(tensor, size_head):
    return tensor.reshape(tensor.shape[0], tensor.shape[1], H, size_head)


def shards_general(queries, key_rows, value_rows, cotangent, lookback, window):
    frames_here, patches_here, model_width = queries.shape
    size_head = model_width // H
    score_scale = 1.0 / math.sqrt(size_head)
    highest = lax.Precision.HIGHEST
    frame_index = lax.axis_index("frame")
    cycle_depth = (LOOK + frames_here - 2) // frames_here
    earlier = []
    carried = (key_rows, value_rows)
    for distance in range(cycle_depth):
        carried = shifted((carried[0], carried[1]), "frame", 1)
        earlier.append(carried)
    bank_keys = jnp.concatenate(
        [earlier[cycle_depth - 1 - number][0] for number in range(cycle_depth)] + [key_rows], axis=0
    )
    bank_values = jnp.concatenate(
        [earlier[cycle_depth - 1 - number][1] for number in range(cycle_depth)] + [value_rows],
        axis=0,
    )
    bank_frames = bank_keys.shape[0]
    q_heads = split_heads(queries, size_head)
    key_heads = split_heads(bank_keys, size_head)
    value_heads = split_heads(bank_values, size_head)
    query_frame = frame_index * frames_here + jnp.arange(frames_here, dtype=jnp.int32)
    key_frame = (frame_index - cycle_depth) * frames_here + jnp.arange(bank_frames, dtype=jnp.int32)
    offset = query_frame[:, None] - key_frame[None, :]
    visible = (offset >= 0) & (offset < lookback[:, None]) & (key_frame[None, :] >= 0)
    scores = jnp.einsum("fphe,jphe->phfj", q_heads, key_heads, precision=highest) * score_scale
    scores = jnp.where(visible, scores, -jnp.inf)
    weights = jax.nn.softmax(scores, axis=-1)
    temporal = jnp.einsum("phfj,jphe->fphe", weights, value_heads, precision=highest).reshape(
        frames_here, patches_here, model_width
    )
    patch_count = lax.axis_size("patch")
    patch_index = lax.axis_index("patch")
    blocks_here = patches_here // BLK
    reach_devices = -(-REACH // blocks_here)
    offsets = []
    for stride in range(-reach_devices, reach_devices + 1):
        if all(((stride - earlier_step) % patch_count != 0 for earlier_step in offsets)):
            offsets.append(stride)
    entries = []
    running_base = 0
    for stride in offsets:
        count_here = blocks_here if stride != 0 and abs(stride) == reach_devices else blocks_here
        first_block = 0 if stride >= 0 else blocks_here - count_here
        entries.append((stride, first_block, count_here, running_base))
        running_base = running_base + count_here
    count_slots = running_base
    near_banks = []
    for stride, first_block, count_here, base_slot in entries:
        rows_from = first_block * BLK
        rows_to = (first_block + count_here) * BLK
        piece = (key_rows, temporal)
        if stride == 0:
            near_banks.append(piece)
        else:
            near_banks.append(passed_along((piece[0], piece[1]), "patch", -stride))
    near_keys = jnp.concatenate([entry[0] for entry in near_banks], axis=1)
    near_values = jnp.concatenate([entry[1] for entry in near_banks], axis=1)
    owner_device = window // blocks_here
    relative = (owner_device - patch_index) % patch_count
    base_of = jnp.zeros(window.shape, jnp.int32)
    first_of = jnp.zeros(window.shape, jnp.int32)
    for stride, first_block, count_here, base_slot in entries:
        matches = relative == stride % patch_count
        base_of = jnp.where(matches, base_slot, base_of)
        first_of = jnp.where(matches, first_block, first_of)
    slot_index = base_of + window % blocks_here - first_of
    window_count = window.shape[1]
    key_blocks = near_keys.reshape(frames_here, count_slots, BLK, model_width)
    value_blocks = near_values.reshape(frames_here, count_slots, BLK, model_width)

    def frame_step(frame_items):
        query_part, key_part, value_part, grad_part = frame_items
        key_win = key_part[slot_index].reshape(blocks_here, window_count * BLK, H, size_head)
        value_win = value_part[slot_index].reshape(blocks_here, window_count * BLK, H, size_head)
        query_win = query_part.reshape(blocks_here, BLK, H, size_head)
        grad_win = grad_part.reshape(blocks_here, BLK, H, size_head)
        logits = jnp.einsum("bxhe,byhe->bhxy", query_win, key_win, precision=highest) * score_scale
        attention = jax.nn.softmax(logits, axis=-1)
        mixed_rows = jnp.einsum("bhxy,byhe->bxhe", attention, value_win, precision=highest)
        grad_attention = jnp.einsum("bxhe,byhe->bhxy", grad_win, value_win, precision=highest)
        grad_logits = attention * (
            grad_attention - jnp.sum(attention * grad_attention, axis=-1, keepdims=True)
        )
        grad_query = (
            jnp.einsum("bhxy,byhe->bxhe", grad_logits, key_win, precision=highest) * score_scale
        )
        grad_key = (
            jnp.einsum("bhxy,bxhe->byhe", grad_logits, query_win, precision=highest) * score_scale
        )
        grad_value = jnp.einsum("bhxy,bxhe->byhe", attention, grad_win, precision=highest)
        block_shape = (blocks_here, window_count, BLK, model_width)
        key_back = (
            jnp.zeros((count_slots, BLK, model_width), jnp.float32)
            .at[slot_index]
            .add(grad_key.reshape(block_shape))
        )
        value_back = (
            jnp.zeros((count_slots, BLK, model_width), jnp.float32)
            .at[slot_index]
            .add(grad_value.reshape(block_shape))
        )
        return (
            mixed_rows.reshape(patches_here, model_width),
            grad_query.reshape(patches_here, model_width),
            key_back,
            value_back,
        )

    mixed, grad_query_space, key_back, value_back = lax.map(
        frame_step, (queries, key_blocks, value_blocks, cotangent)
    )
    key_back = key_back.reshape(frames_here, count_slots * BLK, model_width)
    value_back = value_back.reshape(frames_here, count_slots * BLK, model_width)
    grad_key_space = jnp.zeros(queries.shape, jnp.float32)
    grad_temporal = jnp.zeros(queries.shape, jnp.float32)
    for stride, first_block, count_here, base_slot in entries:
        slot_from = base_slot * BLK
        slot_to = (base_slot + count_here) * BLK
        returned = (key_back[:, slot_from:slot_to], value_back[:, slot_from:slot_to])
        if stride != 0:
            returned = passed_along((returned[0], returned[1]), "patch", stride)
        rows_from = first_block * BLK
        rows_to = (first_block + count_here) * BLK
        grad_key_space = grad_key_space.at[:, rows_from:rows_to].add(returned[0])
        grad_temporal = grad_temporal.at[:, rows_from:rows_to].add(returned[1])
    grad_heads = split_heads(grad_temporal, size_head)
    grad_weights = jnp.einsum("fphe,jphe->phfj", grad_heads, value_heads, precision=highest)
    grad_scores = weights * (grad_weights - jnp.sum(weights * grad_weights, axis=-1, keepdims=True))
    grad_query_time = (
        jnp.einsum("phfj,jphe->fphe", grad_scores, key_heads, precision=highest) * score_scale
    )
    key_terms = (
        jnp.einsum("phfj,fphe->jphe", grad_scores, q_heads, precision=highest) * score_scale
    ).reshape(cycle_depth + 1, frames_here, patches_here, model_width)
    value_terms = jnp.einsum("phfj,fphe->jphe", weights, grad_heads, precision=highest).reshape(
        cycle_depth + 1, frames_here, patches_here, model_width
    )
    carried = (key_terms[0], value_terms[0])
    for distance in range(1, cycle_depth + 1):
        carried = shifted((carried[0], carried[1]), "frame", -1)
        carried = (carried[0] + key_terms[distance], carried[1] + value_terms[distance])
    grad_key_time, grad_value_time = carried
    grad_queries = grad_query_space + grad_query_time.reshape(
        frames_here, patches_here, model_width
    )
    grad_keys = grad_key_space + grad_key_time
    return (mixed, grad_queries, grad_keys, grad_value_time)


LANES = 128
INFO = 8


def swap_halves(x):
    return pltpu.roll(x, LANES // 2, x.ndim - 1)


def interleave(first, second):
    low = lax.broadcasted_iota(jnp.int32, first.shape, first.ndim - 1) < LANES // 2
    return (
        jnp.where(low, first, swap_halves(second)),
        jnp.where(low, swap_halves(first), second),
    )


def pack_kernel(window_ref, lookback_ref, *refs):
    arrays, out_ref = refs[:-1], refs[-1]
    rows = arrays[0].shape[1]
    row = lax.broadcasted_iota(jnp.int32, (INFO, LANES), 0)
    lane = lax.broadcasted_iota(jnp.int32, (INFO, LANES), 1)
    info = jnp.zeros((INFO, LANES), jnp.int32)
    for block in range(rows // BLK):
        for column in range(window_ref.shape[1]):
            at = block * BLK + (column // INFO) * (LANES // 2)
            here = (row == column % INFO) & (lane >= at) & (lane < at + BLK)
            info = jnp.where(here, window_ref[block, column], info)
    for frame in range(2):
        here = (row == INFO - 2 + frame) & (lane >= LANES // 2)
        info = jnp.where(here, lookback_ref[frame], info)
    info = info.astype(jnp.float32)
    for pair in range(H // 2):
        cols = slice(pair * LANES, (pair + 1) * LANES)
        for number, ref in enumerate(arrays):
            at = slice(number * rows, (number + 1) * rows)
            out_ref[2 * pair, at], out_ref[2 * pair + 1, at] = interleave(
                ref[0, :, cols], ref[1, :, cols]
            )
        at = slice(len(arrays) * rows, len(arrays) * rows + INFO)
        out_ref[2 * pair, at] = info
        out_ref[2 * pair + 1, at] = info


def unpack_kernel(in_ref, *out_refs):
    rows = out_refs[0].shape[1]
    for pair in range(H // 2):
        cols = slice(pair * LANES, (pair + 1) * LANES)
        for number, ref in enumerate(out_refs):
            at = slice(number * rows, (number + 1) * rows)
            ref[0, :, cols], ref[1, :, cols] = interleave(
                in_ref[2 * pair, at], in_ref[2 * pair + 1, at]
            )


def dot(a, b, dims):
    return lax.dot_general(
        a, b, (dims, ((), ())), precision=lax.Precision.HIGHEST, preferred_element_type=jnp.float32
    )


NN = ((1,), (0,))
NT = ((1,), (1,))


def head_kernel(
    frames, patches, columns, in_ref, out_ref, qt, kt, vt, ct, tt, tn, gt, gq, gk, gv, wts, bias
):
    rows = (in_ref.shape[1] - INFO) // 4
    size = LANES // 2
    pairs = frames // 2
    parts = patches // rows
    scale = 1.0 / math.sqrt(size)

    def natural(number, pair):
        at = pl.ds(number * rows, rows)
        return in_ref[pl.ds(pair * parts, parts), at].reshape(patches, LANES)

    info = [in_ref[part, 4 * rows : 4 * rows + INFO] for part in range(parts)]
    low = lax.broadcasted_iota(jnp.int32, (INFO, LANES), 1) < LANES // 2
    firsts, lasts = [], []
    for part in range(0, parts, 2):
        first, last = interleave(info[part], info[part + 1])
        firsts.append(first)
        lasts.append(last)
    first = jnp.concatenate(firsts, axis=1)
    last = jnp.concatenate(lasts, axis=1)
    key_block = (lax.broadcasted_iota(jnp.int32, (patches, patches), 0) // BLK).astype(jnp.float32)
    seen = key_block == first[0:1]
    for column in range(1, columns):
        of = first if column < INFO else last
        seen = seen | (key_block == of[column % INFO : column % INFO + 1])
    bias[...] = jnp.where(seen, 0.0, -jnp.inf)

    def turn(pair, carry):
        at = pl.ds(pair * LANES, LANES)
        qt[at] = natural(0, pair).T * scale
        kt[at] = natural(1, pair).T
        vt[at] = natural(2, pair).T
        ct[at] = natural(3, pair).T
        return carry

    lax.fori_loop(0, pairs, turn, 0)

    def frame_rows(ref, frame, cols):
        return ref[frame * size : (frame + 1) * size, cols]

    lookbacks = []
    for frame in range(frames):
        tile = in_ref[(frame // 2) * parts, 4 * rows : 4 * rows + INFO]
        _, tile = interleave(tile, tile)
        lookbacks.append(tile[INFO - 2 + frame % 2 : INFO - 1 + frame % 2])

    for chunk in range(patches // LANES):
        cols = slice(chunk * LANES, (chunk + 1) * LANES)
        for frame in range(frames):
            q = frame_rows(qt, frame, cols)
            keys = range(max(0, frame - LOOK + 1), frame + 1)
            scores = []
            for key in keys:
                score = jnp.sum(q * frame_rows(kt, key, cols), axis=0, keepdims=True)
                gap = float(frame - key)
                scores.append(jnp.where(lookbacks[frame] > gap, score, -jnp.inf))
            top = scores[0]
            for score in scores[1:]:
                top = jnp.maximum(top, score)
            exps = [jnp.exp(score - top) for score in scores]
            total = exps[0]
            for term in exps[1:]:
                total = total + term
            value = jnp.zeros((size, LANES), jnp.float32)
            for key, term in zip(keys, exps):
                weight = term / total
                wts[frame, frame - key : frame - key + 1, cols] = weight
                value = value + weight * frame_rows(vt, key, cols)
            tt[frame * size : (frame + 1) * size, cols] = value

    def spatial(pair, carry):
        at = pl.ds(pair * LANES, LANES)
        tn[...] = tt[at].T
        keys = natural(1, pair)
        zeros = jnp.zeros((size, patches), jnp.float32)
        mixed = []
        for half in range(2):
            mine = pl.ds(pair * LANES + half * size, size)

            def padded(x):
                return jnp.concatenate([x, zeros] if half == 0 else [zeros, x], axis=0)

            logits = dot(keys, padded(qt[mine]), NN) + bias[...]
            top = jnp.max(logits, axis=0, keepdims=True)
            weights = jnp.exp(logits - top)
            weights = weights / jnp.sum(weights, axis=0, keepdims=True)
            mix = dot(tt[mine], weights, NN)
            mixed.append(mix)
            grad = ct[mine]
            delta = jnp.sum(grad * mix, axis=0, keepdims=True)
            grad_logits = weights * (dot(tn[...], padded(grad), NN) - delta)
            gq[mine] = dot(kt[mine], grad_logits, NN)
            gk[mine] = dot(qt[mine], grad_logits, NT)
            gt[mine] = dot(grad, weights, NT)
        mixed = jnp.concatenate(mixed, axis=0).T.reshape(parts, rows, LANES)
        out_ref[pl.ds(pair * parts, parts), pl.ds(0, rows)] = mixed
        return carry

    lax.fori_loop(0, pairs, spatial, 0)

    gv[...] = jnp.zeros(gv.shape, jnp.float32)
    for chunk in range(patches // LANES):
        cols = slice(chunk * LANES, (chunk + 1) * LANES)
        for frame in range(frames):
            mine = slice(frame * size, (frame + 1) * size)
            q = frame_rows(qt, frame, cols)
            grad = frame_rows(gt, frame, cols)
            keys = range(max(0, frame - LOOK + 1), frame + 1)
            weights, grads = [], []
            inner = jnp.zeros((1, LANES), jnp.float32)
            for key in keys:
                weight = wts[frame, frame - key : frame - key + 1, cols]
                term = jnp.sum(grad * frame_rows(vt, key, cols), axis=0, keepdims=True)
                inner = inner + weight * term
                weights.append(weight)
                grads.append(term)
            grad_q = gq[mine, cols]
            for key, weight, term in zip(keys, weights, grads):
                of = slice(key * size, (key + 1) * size)
                score = weight * (term - inner)
                grad_q = grad_q + score * kt[of, cols]
                gk[of, cols] = gk[of, cols] + score * q
                gv[of, cols] = gv[of, cols] + weight * grad
            gq[mine, cols] = grad_q * scale

    def turn_back(pair, carry):
        at = pl.ds(pair * LANES, LANES)
        for number, ref in ((1, gq), (2, gk), (3, gv)):
            out_ref[pl.ds(pair * parts, parts), pl.ds(number * rows, rows)] = (
                ref[at].T.reshape(parts, rows, LANES)
            )
        return carry

    lax.fori_loop(0, pairs, turn_back, 0)


def shards_by_head(queries, key_rows, value_rows, cotangent, lookback, window):
    frames_here, patches_here, model_width = queries.shape
    group = ("frame", "patch")
    frames = frames_here * lax.axis_size("frame")
    patches = patches_here * lax.axis_size("patch")
    vmem = pl.BlockSpec(memory_space=pltpu.VMEM)
    smem = pl.BlockSpec(memory_space=pltpu.SMEM)
    params = pltpu.CompilerParams(vmem_limit_bytes=40 * 1024 * 1024)
    packed = pl.pallas_call(
        pack_kernel,
        out_shape=jax.ShapeDtypeStruct((H, 4 * patches_here + INFO, LANES), jnp.float32),
        in_specs=[smem, smem] + [vmem] * 4,
        out_specs=vmem,
        compiler_params=params,
        name="pack_heads",
    )(window, lookback, queries, key_rows, value_rows, cotangent)
    by_head = lax.all_to_all(packed, group, 0, 0, tiled=True)
    whole = pltpu.VMEM((frames * LANES // 2, patches), jnp.float32)
    done = pl.pallas_call(
        lambda *refs: head_kernel(frames, patches, window.shape[1], *refs),
        out_shape=jax.ShapeDtypeStruct((H, 4 * patches_here, LANES), jnp.float32),
        in_specs=[vmem],
        out_specs=vmem,
        scratch_shapes=[whole] * 5
        + [pltpu.VMEM((patches, LANES), jnp.float32)]
        + [whole] * 4
        + [pltpu.VMEM((frames, 8, patches), jnp.float32)]
        + [pltpu.VMEM((patches, patches), jnp.float32)],
        compiler_params=params,
        name="one_head",
    )(by_head)
    by_rows = lax.all_to_all(done, group, 0, 0, tiled=True)
    return pl.pallas_call(
        unpack_kernel,
        out_shape=[jax.ShapeDtypeStruct(queries.shape, jnp.float32)] * 4,
        in_specs=[vmem],
        out_specs=[vmem] * 4,
        compiler_params=params,
        name="unpack_heads",
    )(by_rows)


def shards(queries, key_rows, value_rows, cotangent, lookback, window):
    frames_here, patches_here, model_width = queries.shape
    fits = (
        lax.axis_size("frame") * lax.axis_size("patch") == H
        and frames_here == 2
        and patches_here == LANES // 2
        and lax.axis_size("patch") % 2 == 0
        and model_width == H * (LANES // 2)
    )
    form = shards_by_head if fits else shards_general
    return tuple(form(queries, key_rows, value_rows, cotangent, lookback, window))


def solution(mesh):
    in_specs = (
        P(("traj", "frame"), "patch", None),
        P(("traj", "frame"), "patch", None),
        P(("traj", "frame"), "patch", None),
        P(("traj", "frame"), "patch", None),
        P(("traj", "frame")),
        P(("traj", "patch"), None),
    )
    out_specs = (
        P(("traj", "frame"), "patch", None),
        P(("traj", "frame"), "patch", None),
        P(("traj", "frame"), "patch", None),
        P(("traj", "frame"), "patch", None),
    )
    return jax.shard_map(shards, mesh=mesh, in_specs=in_specs, out_specs=out_specs, check_vma=False)
```

```python
import math

import jax
import jax.numpy as jnp
from jax import lax
from jax.experimental import pallas as pl
from jax.experimental.pallas import tpu as pltpu
from jax.sharding import PartitionSpec as P

H = 16
BLK = 16
LOOK = 6
REACH = 6


def shifted(x, axis, by):
    count = lax.axis_size(axis)
    pairs = [(i, i + by) for i in range(count) if 0 <= i + by < count]
    return lax.ppermute(x, axis, pairs)


def passed_along(block, axis, distance):
    devices = range(lax.axis_size(axis))
    route = [((i - distance) % len(devices), i) for i in devices]
    return lax.ppermute(block, axis, route)


def split_heads(tensor, size_head):
    return tensor.reshape(tensor.shape[0], tensor.shape[1], H, size_head)


def shards_general(queries, key_rows, value_rows, cotangent, lookback, window):
    frames_here, patches_here, model_width = queries.shape
    size_head = model_width // H
    score_scale = 1.0 / math.sqrt(size_head)
    highest = lax.Precision.HIGHEST
    frame_index = lax.axis_index("frame")
    cycle_depth = (LOOK + frames_here - 2) // frames_here
    earlier = []
    carried = (key_rows, value_rows)
    for distance in range(cycle_depth):
        carried = shifted((carried[0], carried[1]), "frame", 1)
        earlier.append(carried)
    bank_keys = jnp.concatenate(
        [earlier[cycle_depth - 1 - number][0] for number in range(cycle_depth)] + [key_rows], axis=0
    )
    bank_values = jnp.concatenate(
        [earlier[cycle_depth - 1 - number][1] for number in range(cycle_depth)] + [value_rows],
        axis=0,
    )
    bank_frames = bank_keys.shape[0]
    q_heads = split_heads(queries, size_head)
    key_heads = split_heads(bank_keys, size_head)
    value_heads = split_heads(bank_values, size_head)
    query_frame = frame_index * frames_here + jnp.arange(frames_here, dtype=jnp.int32)
    key_frame = (frame_index - cycle_depth) * frames_here + jnp.arange(bank_frames, dtype=jnp.int32)
    offset = query_frame[:, None] - key_frame[None, :]
    visible = (offset >= 0) & (offset < lookback[:, None]) & (key_frame[None, :] >= 0)
    scores = jnp.einsum("fphe,jphe->phfj", q_heads, key_heads, precision=highest) * score_scale
    scores = jnp.where(visible, scores, -jnp.inf)
    weights = jax.nn.softmax(scores, axis=-1)
    temporal = jnp.einsum("phfj,jphe->fphe", weights, value_heads, precision=highest).reshape(
        frames_here, patches_here, model_width
    )
    patch_count = lax.axis_size("patch")
    patch_index = lax.axis_index("patch")
    blocks_here = patches_here // BLK
    reach_devices = -(-REACH // blocks_here)
    offsets = []
    for stride in range(-reach_devices, reach_devices + 1):
        if all(((stride - earlier_step) % patch_count != 0 for earlier_step in offsets)):
            offsets.append(stride)
    entries = []
    running_base = 0
    for stride in offsets:
        count_here = blocks_here if stride != 0 and abs(stride) == reach_devices else blocks_here
        first_block = 0 if stride >= 0 else blocks_here - count_here
        entries.append((stride, first_block, count_here, running_base))
        running_base = running_base + count_here
    count_slots = running_base
    near_banks = []
    for stride, first_block, count_here, base_slot in entries:
        rows_from = first_block * BLK
        rows_to = (first_block + count_here) * BLK
        piece = (key_rows, temporal)
        if stride == 0:
            near_banks.append(piece)
        else:
            near_banks.append(passed_along((piece[0], piece[1]), "patch", -stride))
    near_keys = jnp.concatenate([entry[0] for entry in near_banks], axis=1)
    near_values = jnp.concatenate([entry[1] for entry in near_banks], axis=1)
    owner_device = window // blocks_here
    relative = (owner_device - patch_index) % patch_count
    base_of = jnp.zeros(window.shape, jnp.int32)
    first_of = jnp.zeros(window.shape, jnp.int32)
    for stride, first_block, count_here, base_slot in entries:
        matches = relative == stride % patch_count
        base_of = jnp.where(matches, base_slot, base_of)
        first_of = jnp.where(matches, first_block, first_of)
    slot_index = base_of + window % blocks_here - first_of
    window_count = window.shape[1]
    key_blocks = near_keys.reshape(frames_here, count_slots, BLK, model_width)
    value_blocks = near_values.reshape(frames_here, count_slots, BLK, model_width)

    def frame_step(frame_items):
        query_part, key_part, value_part, grad_part = frame_items
        key_win = key_part[slot_index].reshape(blocks_here, window_count * BLK, H, size_head)
        value_win = value_part[slot_index].reshape(blocks_here, window_count * BLK, H, size_head)
        query_win = query_part.reshape(blocks_here, BLK, H, size_head)
        grad_win = grad_part.reshape(blocks_here, BLK, H, size_head)
        logits = jnp.einsum("bxhe,byhe->bhxy", query_win, key_win, precision=highest) * score_scale
        attention = jax.nn.softmax(logits, axis=-1)
        mixed_rows = jnp.einsum("bhxy,byhe->bxhe", attention, value_win, precision=highest)
        grad_attention = jnp.einsum("bxhe,byhe->bhxy", grad_win, value_win, precision=highest)
        grad_logits = attention * (
            grad_attention - jnp.sum(attention * grad_attention, axis=-1, keepdims=True)
        )
        grad_query = (
            jnp.einsum("bhxy,byhe->bxhe", grad_logits, key_win, precision=highest) * score_scale
        )
        grad_key = (
            jnp.einsum("bhxy,bxhe->byhe", grad_logits, query_win, precision=highest) * score_scale
        )
        grad_value = jnp.einsum("bhxy,bxhe->byhe", attention, grad_win, precision=highest)
        block_shape = (blocks_here, window_count, BLK, model_width)
        key_back = (
            jnp.zeros((count_slots, BLK, model_width), jnp.float32)
            .at[slot_index]
            .add(grad_key.reshape(block_shape))
        )
        value_back = (
            jnp.zeros((count_slots, BLK, model_width), jnp.float32)
            .at[slot_index]
            .add(grad_value.reshape(block_shape))
        )
        return (
            mixed_rows.reshape(patches_here, model_width),
            grad_query.reshape(patches_here, model_width),
            key_back,
            value_back,
        )

    mixed, grad_query_space, key_back, value_back = lax.map(
        frame_step, (queries, key_blocks, value_blocks, cotangent)
    )
    key_back = key_back.reshape(frames_here, count_slots * BLK, model_width)
    value_back = value_back.reshape(frames_here, count_slots * BLK, model_width)
    grad_key_space = jnp.zeros(queries.shape, jnp.float32)
    grad_temporal = jnp.zeros(queries.shape, jnp.float32)
    for stride, first_block, count_here, base_slot in entries:
        slot_from = base_slot * BLK
        slot_to = (base_slot + count_here) * BLK
        returned = (key_back[:, slot_from:slot_to], value_back[:, slot_from:slot_to])
        if stride != 0:
            returned = passed_along((returned[0], returned[1]), "patch", stride)
        rows_from = first_block * BLK
        rows_to = (first_block + count_here) * BLK
        grad_key_space = grad_key_space.at[:, rows_from:rows_to].add(returned[0])
        grad_temporal = grad_temporal.at[:, rows_from:rows_to].add(returned[1])
    grad_heads = split_heads(grad_temporal, size_head)
    grad_weights = jnp.einsum("fphe,jphe->phfj", grad_heads, value_heads, precision=highest)
    grad_scores = weights * (grad_weights - jnp.sum(weights * grad_weights, axis=-1, keepdims=True))
    grad_query_time = (
        jnp.einsum("phfj,jphe->fphe", grad_scores, key_heads, precision=highest) * score_scale
    )
    key_terms = (
        jnp.einsum("phfj,fphe->jphe", grad_scores, q_heads, precision=highest) * score_scale
    ).reshape(cycle_depth + 1, frames_here, patches_here, model_width)
    value_terms = jnp.einsum("phfj,fphe->jphe", weights, grad_heads, precision=highest).reshape(
        cycle_depth + 1, frames_here, patches_here, model_width
    )
    carried = (key_terms[0], value_terms[0])
    for distance in range(1, cycle_depth + 1):
        carried = shifted((carried[0], carried[1]), "frame", -1)
        carried = (carried[0] + key_terms[distance], carried[1] + value_terms[distance])
    grad_key_time, grad_value_time = carried
    grad_queries = grad_query_space + grad_query_time.reshape(
        frames_here, patches_here, model_width
    )
    grad_keys = grad_key_space + grad_key_time
    return (mixed, grad_queries, grad_keys, grad_value_time)


LANES = 128
INFO = 8


def swap_halves(x):
    return pltpu.roll(x, LANES // 2, x.ndim - 1)


def interleave(first, second):
    low = lax.broadcasted_iota(jnp.int32, first.shape, first.ndim - 1) < LANES // 2
    return (
        jnp.where(low, first, swap_halves(second)),
        jnp.where(low, swap_halves(first), second),
    )


def pack_kernel(window_ref, lookback_ref, *refs):
    arrays, out_ref = refs[:-1], refs[-1]
    rows = arrays[0].shape[1]
    row = lax.broadcasted_iota(jnp.int32, (INFO, LANES), 0)
    lane = lax.broadcasted_iota(jnp.int32, (INFO, LANES), 1)
    info = jnp.zeros((INFO, LANES), jnp.int32)
    for block in range(rows // BLK):
        for column in range(window_ref.shape[1]):
            at = block * BLK + (column // INFO) * (LANES // 2)
            here = (row == column % INFO) & (lane >= at) & (lane < at + BLK)
            info = jnp.where(here, window_ref[block, column], info)
    for frame in range(2):
        here = (row == INFO - 2 + frame) & (lane >= LANES // 2)
        info = jnp.where(here, lookback_ref[frame], info)
    info = info.astype(jnp.float32)
    for pair in range(H // 2):
        cols = slice(pair * LANES, (pair + 1) * LANES)
        for number, ref in enumerate(arrays):
            at = slice(number * rows, (number + 1) * rows)
            out_ref[2 * pair, at], out_ref[2 * pair + 1, at] = interleave(
                ref[0, :, cols], ref[1, :, cols]
            )
        at = slice(len(arrays) * rows, len(arrays) * rows + INFO)
        out_ref[2 * pair, at] = info
        out_ref[2 * pair + 1, at] = info


def unpack_kernel(in_ref, *out_refs):
    rows = out_refs[0].shape[1]
    for pair in range(H // 2):
        cols = slice(pair * LANES, (pair + 1) * LANES)
        for number, ref in enumerate(out_refs):
            at = slice(number * rows, (number + 1) * rows)
            ref[0, :, cols], ref[1, :, cols] = interleave(
                in_ref[2 * pair, at], in_ref[2 * pair + 1, at]
            )


def dot(a, b, dims):
    return lax.dot_general(a, b, (dims, ((), ())), preferred_element_type=jnp.float32)


def split(x):
    high = x.astype(jnp.bfloat16)
    return high, (x - high.astype(jnp.float32)).astype(jnp.bfloat16)


def stacked(x, times):
    high, low = split(x)
    return jnp.concatenate([high] * times + [low] * times, axis=0)


def heads_dot(x, high, low, dims):
    both = stacked(x, 1)
    size = x.shape[0]
    out = dot(both, high, dims)
    return out[:size] + (out[size:] + dot(both[:size], low, dims))


NN = ((1,), (0,))
NT = ((1,), (1,))


def head_kernel(
    frames, patches, columns, in_ref, out_ref, qt, kt, vt, ct, tt, gt, gq, gk, gv, wts, bias
):
    rows = (in_ref.shape[1] - INFO) // 4
    size = LANES // 2
    pairs = frames // 2
    parts = patches // rows
    scale = 1.0 / math.sqrt(size)

    def natural(number, pair):
        at = pl.ds(number * rows, rows)
        return in_ref[pl.ds(pair * parts, parts), at].reshape(patches, LANES)

    info = [in_ref[part, 4 * rows : 4 * rows + INFO] for part in range(parts)]
    low = lax.broadcasted_iota(jnp.int32, (INFO, LANES), 1) < LANES // 2
    firsts, lasts = [], []
    for part in range(0, parts, 2):
        first, last = interleave(info[part], info[part + 1])
        firsts.append(first)
        lasts.append(last)
    first = jnp.concatenate(firsts, axis=1)
    last = jnp.concatenate(lasts, axis=1)
    key_block = (lax.broadcasted_iota(jnp.int32, (patches, patches), 0) // BLK).astype(jnp.float32)
    seen = key_block == first[0:1]
    for column in range(1, columns):
        of = first if column < INFO else last
        seen = seen | (key_block == of[column % INFO : column % INFO + 1])
    bias[...] = jnp.where(seen, 0.0, -jnp.inf)

    def turn(pair, carry):
        at = pl.ds(pair * LANES, LANES)
        qt[at] = natural(0, pair).T * scale
        kt[at] = natural(1, pair).T
        vt[at] = natural(2, pair).T
        ct[at] = natural(3, pair).T
        return carry

    lax.fori_loop(0, pairs, turn, 0, unroll=True)

    def halves(x):
        high = x.astype(jnp.bfloat16).astype(jnp.float32)
        sides = interleave(high, x - high)
        return [jnp.concatenate([side.astype(jnp.bfloat16)] * 2, axis=1) for side in sides]

    def frame_rows(ref, frame, cols):
        return ref[frame * size : (frame + 1) * size, cols]

    lookbacks = []
    for frame in range(frames):
        tile = in_ref[(frame // 2) * parts, 4 * rows : 4 * rows + INFO]
        _, tile = interleave(tile, tile)
        lookbacks.append(tile[INFO - 2 + frame % 2 : INFO - 1 + frame % 2])

    for chunk in range(patches // LANES):
        cols = slice(chunk * LANES, (chunk + 1) * LANES)
        for frame in range(frames):
            q = frame_rows(qt, frame, cols)
            keys = range(max(0, frame - LOOK + 1), frame + 1)
            scores = []
            for key in keys:
                score = jnp.sum(q * frame_rows(kt, key, cols), axis=0, keepdims=True)
                gap = float(frame - key)
                scores.append(jnp.where(lookbacks[frame] > gap, score, -jnp.inf))
            top = scores[0]
            for score in scores[1:]:
                top = jnp.maximum(top, score)
            exps = [jnp.exp(score - top) for score in scores]
            total = exps[0]
            for term in exps[1:]:
                total = total + term
            value = jnp.zeros((size, LANES), jnp.float32)
            for key, term in zip(keys, exps):
                weight = term / total
                wts[frame, frame - key : frame - key + 1, cols] = weight
                value = value + weight * frame_rows(vt, key, cols)
            tt[frame * size : (frame + 1) * size, cols] = value

    def spatial(pair, carry):
        at = pl.ds(pair * LANES, LANES)
        keys = halves(natural(1, pair))
        values = halves(tt[at].T)
        mixed = []
        for half in range(2):
            mine = pl.ds(pair * LANES + half * size, size)
            query, grad = qt[mine], ct[mine]
            logits = dot(keys[half], stacked(query, 2), NN) + bias[...]
            grad_weights = dot(values[half], stacked(grad, 2), NN)
            top = jnp.max(logits, axis=0, keepdims=True)
            exps = jnp.exp(logits - top)
            share = 1.0 / jnp.sum(exps, axis=0, keepdims=True)
            high, low = split(exps)
            mix = heads_dot(tt[mine], high, low, NN) * share
            mixed.append(mix)
            gt[mine] = heads_dot(grad * share, high, low, NT)
            delta = jnp.sum(grad * mix, axis=0, keepdims=True)
            high, low = split(exps * (grad_weights - delta))
            gq[mine] = heads_dot(kt[mine], high, low, NN) * share
            gk[mine] = heads_dot(query * share, high, low, NT)
        mixed = jnp.concatenate(mixed, axis=0).T.reshape(parts, rows, LANES)
        out_ref[pl.ds(pair * parts, parts), pl.ds(0, rows)] = mixed
        return carry

    lax.fori_loop(0, pairs, spatial, 0, unroll=True)

    gv[...] = jnp.zeros(gv.shape, jnp.float32)
    for chunk in range(patches // LANES):
        cols = slice(chunk * LANES, (chunk + 1) * LANES)
        for frame in range(frames):
            mine = slice(frame * size, (frame + 1) * size)
            q = frame_rows(qt, frame, cols)
            grad = frame_rows(gt, frame, cols)
            keys = range(max(0, frame - LOOK + 1), frame + 1)
            weights, grads = [], []
            inner = jnp.zeros((1, LANES), jnp.float32)
            for key in keys:
                weight = wts[frame, frame - key : frame - key + 1, cols]
                term = jnp.sum(grad * frame_rows(vt, key, cols), axis=0, keepdims=True)
                inner = inner + weight * term
                weights.append(weight)
                grads.append(term)
            grad_q = gq[mine, cols]
            for key, weight, term in zip(keys, weights, grads):
                of = slice(key * size, (key + 1) * size)
                score = weight * (term - inner)
                grad_q = grad_q + score * kt[of, cols]
                gk[of, cols] = gk[of, cols] + score * q
                gv[of, cols] = gv[of, cols] + weight * grad
            gq[mine, cols] = grad_q * scale

    def turn_back(pair, carry):
        at = pl.ds(pair * LANES, LANES)
        for number, ref in ((1, gq), (2, gk), (3, gv)):
            out_ref[pl.ds(pair * parts, parts), pl.ds(number * rows, rows)] = (
                ref[at].T.reshape(parts, rows, LANES)
            )
        return carry

    lax.fori_loop(0, pairs, turn_back, 0, unroll=True)


def shards_by_head(queries, key_rows, value_rows, cotangent, lookback, window):
    frames_here, patches_here, model_width = queries.shape
    group = ("frame", "patch")
    frames = frames_here * lax.axis_size("frame")
    patches = patches_here * lax.axis_size("patch")
    vmem = pl.BlockSpec(memory_space=pltpu.VMEM)
    smem = pl.BlockSpec(memory_space=pltpu.SMEM)
    params = pltpu.CompilerParams(vmem_limit_bytes=40 * 1024 * 1024)
    packed = pl.pallas_call(
        pack_kernel,
        out_shape=jax.ShapeDtypeStruct((H, 4 * patches_here + INFO, LANES), jnp.float32),
        in_specs=[smem, smem] + [vmem] * 4,
        out_specs=vmem,
        compiler_params=params,
        name="pack_heads",
    )(window, lookback, queries, key_rows, value_rows, cotangent)
    by_head = lax.all_to_all(packed, group, 0, 0, tiled=True)
    whole = pltpu.VMEM((frames * LANES // 2, patches), jnp.float32)
    done = pl.pallas_call(
        lambda *refs: head_kernel(frames, patches, window.shape[1], *refs),
        out_shape=jax.ShapeDtypeStruct((H, 4 * patches_here, LANES), jnp.float32),
        in_specs=[vmem],
        out_specs=vmem,
        scratch_shapes=[whole] * 9
        + [pltpu.VMEM((frames, 8, patches), jnp.float32)]
        + [pltpu.VMEM((patches, patches), jnp.float32)],
        compiler_params=params,
        name="one_head",
    )(by_head)
    by_rows = lax.all_to_all(done, group, 0, 0, tiled=True)
    return pl.pallas_call(
        unpack_kernel,
        out_shape=[jax.ShapeDtypeStruct(queries.shape, jnp.float32)] * 4,
        in_specs=[vmem],
        out_specs=[vmem] * 4,
        compiler_params=params,
        name="unpack_heads",
    )(by_rows)


def shards(queries, key_rows, value_rows, cotangent, lookback, window):
    frames_here, patches_here, model_width = queries.shape
    fits = (
        lax.axis_size("frame") * lax.axis_size("patch") == H
        and frames_here == 2
        and patches_here == LANES // 2
        and lax.axis_size("patch") % 2 == 0
        and model_width == H * (LANES // 2)
    )
    form = shards_by_head if fits else shards_general
    return tuple(form(queries, key_rows, value_rows, cotangent, lookback, window))


def solution(mesh):
    in_specs = (
        P(("traj", "frame"), "patch", None),
        P(("traj", "frame"), "patch", None),
        P(("traj", "frame"), "patch", None),
        P(("traj", "frame"), "patch", None),
        P(("traj", "frame")),
        P(("traj", "patch"), None),
    )
    out_specs = (
        P(("traj", "frame"), "patch", None),
        P(("traj", "frame"), "patch", None),
        P(("traj", "frame"), "patch", None),
        P(("traj", "frame"), "patch", None),
    )
    return jax.shard_map(shards, mesh=mesh, in_specs=in_specs, out_specs=out_specs, check_vma=False)
```

```python
import math

import jax
import jax.numpy as jnp
from jax import lax
from jax.experimental import pallas as pl
from jax.experimental.pallas import tpu as pltpu
from jax.sharding import PartitionSpec as P

H = 16
BLK = 16
LOOK = 6
REACH = 6


def shifted(x, axis, by):
    count = lax.axis_size(axis)
    pairs = [(i, i + by) for i in range(count) if 0 <= i + by < count]
    return lax.ppermute(x, axis, pairs)


def passed_along(block, axis, distance):
    devices = range(lax.axis_size(axis))
    route = [((i - distance) % len(devices), i) for i in devices]
    return lax.ppermute(block, axis, route)


def split_heads(tensor, size_head):
    return tensor.reshape(tensor.shape[0], tensor.shape[1], H, size_head)


def shards_general(queries, key_rows, value_rows, cotangent, lookback, window):
    frames_here, patches_here, model_width = queries.shape
    size_head = model_width // H
    score_scale = 1.0 / math.sqrt(size_head)
    highest = lax.Precision.HIGHEST
    frame_index = lax.axis_index("frame")
    cycle_depth = (LOOK + frames_here - 2) // frames_here
    earlier = []
    carried = (key_rows, value_rows)
    for distance in range(cycle_depth):
        carried = shifted((carried[0], carried[1]), "frame", 1)
        earlier.append(carried)
    bank_keys = jnp.concatenate(
        [earlier[cycle_depth - 1 - number][0] for number in range(cycle_depth)] + [key_rows], axis=0
    )
    bank_values = jnp.concatenate(
        [earlier[cycle_depth - 1 - number][1] for number in range(cycle_depth)] + [value_rows],
        axis=0,
    )
    bank_frames = bank_keys.shape[0]
    q_heads = split_heads(queries, size_head)
    key_heads = split_heads(bank_keys, size_head)
    value_heads = split_heads(bank_values, size_head)
    query_frame = frame_index * frames_here + jnp.arange(frames_here, dtype=jnp.int32)
    key_frame = (frame_index - cycle_depth) * frames_here + jnp.arange(bank_frames, dtype=jnp.int32)
    offset = query_frame[:, None] - key_frame[None, :]
    visible = (offset >= 0) & (offset < lookback[:, None]) & (key_frame[None, :] >= 0)
    scores = jnp.einsum("fphe,jphe->phfj", q_heads, key_heads, precision=highest) * score_scale
    scores = jnp.where(visible, scores, -jnp.inf)
    weights = jax.nn.softmax(scores, axis=-1)
    temporal = jnp.einsum("phfj,jphe->fphe", weights, value_heads, precision=highest).reshape(
        frames_here, patches_here, model_width
    )
    patch_count = lax.axis_size("patch")
    patch_index = lax.axis_index("patch")
    blocks_here = patches_here // BLK
    reach_devices = -(-REACH // blocks_here)
    offsets = []
    for stride in range(-reach_devices, reach_devices + 1):
        if all(((stride - earlier_step) % patch_count != 0 for earlier_step in offsets)):
            offsets.append(stride)
    entries = []
    running_base = 0
    for stride in offsets:
        count_here = blocks_here if stride != 0 and abs(stride) == reach_devices else blocks_here
        first_block = 0 if stride >= 0 else blocks_here - count_here
        entries.append((stride, first_block, count_here, running_base))
        running_base = running_base + count_here
    count_slots = running_base
    near_banks = []
    for stride, first_block, count_here, base_slot in entries:
        rows_from = first_block * BLK
        rows_to = (first_block + count_here) * BLK
        piece = (key_rows, temporal)
        if stride == 0:
            near_banks.append(piece)
        else:
            near_banks.append(passed_along((piece[0], piece[1]), "patch", -stride))
    near_keys = jnp.concatenate([entry[0] for entry in near_banks], axis=1)
    near_values = jnp.concatenate([entry[1] for entry in near_banks], axis=1)
    owner_device = window // blocks_here
    relative = (owner_device - patch_index) % patch_count
    base_of = jnp.zeros(window.shape, jnp.int32)
    first_of = jnp.zeros(window.shape, jnp.int32)
    for stride, first_block, count_here, base_slot in entries:
        matches = relative == stride % patch_count
        base_of = jnp.where(matches, base_slot, base_of)
        first_of = jnp.where(matches, first_block, first_of)
    slot_index = base_of + window % blocks_here - first_of
    window_count = window.shape[1]
    key_blocks = near_keys.reshape(frames_here, count_slots, BLK, model_width)
    value_blocks = near_values.reshape(frames_here, count_slots, BLK, model_width)

    def frame_step(frame_items):
        query_part, key_part, value_part, grad_part = frame_items
        key_win = key_part[slot_index].reshape(blocks_here, window_count * BLK, H, size_head)
        value_win = value_part[slot_index].reshape(blocks_here, window_count * BLK, H, size_head)
        query_win = query_part.reshape(blocks_here, BLK, H, size_head)
        grad_win = grad_part.reshape(blocks_here, BLK, H, size_head)
        logits = jnp.einsum("bxhe,byhe->bhxy", query_win, key_win, precision=highest) * score_scale
        attention = jax.nn.softmax(logits, axis=-1)
        mixed_rows = jnp.einsum("bhxy,byhe->bxhe", attention, value_win, precision=highest)
        grad_attention = jnp.einsum("bxhe,byhe->bhxy", grad_win, value_win, precision=highest)
        grad_logits = attention * (
            grad_attention - jnp.sum(attention * grad_attention, axis=-1, keepdims=True)
        )
        grad_query = (
            jnp.einsum("bhxy,byhe->bxhe", grad_logits, key_win, precision=highest) * score_scale
        )
        grad_key = (
            jnp.einsum("bhxy,bxhe->byhe", grad_logits, query_win, precision=highest) * score_scale
        )
        grad_value = jnp.einsum("bhxy,bxhe->byhe", attention, grad_win, precision=highest)
        block_shape = (blocks_here, window_count, BLK, model_width)
        key_back = (
            jnp.zeros((count_slots, BLK, model_width), jnp.float32)
            .at[slot_index]
            .add(grad_key.reshape(block_shape))
        )
        value_back = (
            jnp.zeros((count_slots, BLK, model_width), jnp.float32)
            .at[slot_index]
            .add(grad_value.reshape(block_shape))
        )
        return (
            mixed_rows.reshape(patches_here, model_width),
            grad_query.reshape(patches_here, model_width),
            key_back,
            value_back,
        )

    mixed, grad_query_space, key_back, value_back = lax.map(
        frame_step, (queries, key_blocks, value_blocks, cotangent)
    )
    key_back = key_back.reshape(frames_here, count_slots * BLK, model_width)
    value_back = value_back.reshape(frames_here, count_slots * BLK, model_width)
    grad_key_space = jnp.zeros(queries.shape, jnp.float32)
    grad_temporal = jnp.zeros(queries.shape, jnp.float32)
    for stride, first_block, count_here, base_slot in entries:
        slot_from = base_slot * BLK
        slot_to = (base_slot + count_here) * BLK
        returned = (key_back[:, slot_from:slot_to], value_back[:, slot_from:slot_to])
        if stride != 0:
            returned = passed_along((returned[0], returned[1]), "patch", stride)
        rows_from = first_block * BLK
        rows_to = (first_block + count_here) * BLK
        grad_key_space = grad_key_space.at[:, rows_from:rows_to].add(returned[0])
        grad_temporal = grad_temporal.at[:, rows_from:rows_to].add(returned[1])
    grad_heads = split_heads(grad_temporal, size_head)
    grad_weights = jnp.einsum("fphe,jphe->phfj", grad_heads, value_heads, precision=highest)
    grad_scores = weights * (grad_weights - jnp.sum(weights * grad_weights, axis=-1, keepdims=True))
    grad_query_time = (
        jnp.einsum("phfj,jphe->fphe", grad_scores, key_heads, precision=highest) * score_scale
    )
    key_terms = (
        jnp.einsum("phfj,fphe->jphe", grad_scores, q_heads, precision=highest) * score_scale
    ).reshape(cycle_depth + 1, frames_here, patches_here, model_width)
    value_terms = jnp.einsum("phfj,fphe->jphe", weights, grad_heads, precision=highest).reshape(
        cycle_depth + 1, frames_here, patches_here, model_width
    )
    carried = (key_terms[0], value_terms[0])
    for distance in range(1, cycle_depth + 1):
        carried = shifted((carried[0], carried[1]), "frame", -1)
        carried = (carried[0] + key_terms[distance], carried[1] + value_terms[distance])
    grad_key_time, grad_value_time = carried
    grad_queries = grad_query_space + grad_query_time.reshape(
        frames_here, patches_here, model_width
    )
    grad_keys = grad_key_space + grad_key_time
    return (mixed, grad_queries, grad_keys, grad_value_time)


LANES = 128
SIZE = LANES // 2
INFO = 8
NN = ((1,), (0,))
NT = ((1,), (1,))


def interleave(first, second):
    axis = first.ndim - 1
    low = lax.broadcasted_iota(jnp.int32, first.shape, axis) < SIZE
    return (
        jnp.where(low, first, pltpu.roll(second, SIZE, axis)),
        jnp.where(low, pltpu.roll(first, SIZE, axis), second),
    )


def dot(a, b, dims):
    return lax.dot_general(a, b, (dims, ((), ())), preferred_element_type=jnp.float32)


def split(x):
    high = x.astype(jnp.bfloat16)
    return high, (x - high.astype(jnp.float32)).astype(jnp.bfloat16)


def stacked(x, times):
    high, low = split(x)
    return jnp.concatenate([high] * times + [low] * times, axis=0)


def heads_dot(x, high, low, dims):
    both = stacked(x, 1)
    out = dot(both, high, dims)
    return out[:SIZE] + (out[SIZE:] + dot(both[:SIZE], low, dims))


def partners(frame_count, patch_count):
    return [(frame, patch) for frame in range(frame_count) for patch in range(patch_count)]


def place(partner, patch_count):
    frame = lax.bitwise_xor(lax.axis_index("frame"), partner[0])
    return frame * patch_count + lax.bitwise_xor(lax.axis_index("patch"), partner[1])


def pack_kernel(order, patch_count, window, lookback, *refs):
    arrays, out_refs = refs[:4], refs[4 : 4 + H]
    held, (packed, window_ref, lookback_ref, sems) = refs[4 + H : 8 + H], refs[8 + H :]
    moves = list(zip((*arrays, window, lookback), (*held, window_ref, lookback_ref)))
    copies = [pltpu.make_async_copy(a, b, sems.at[n]) for n, (a, b) in enumerate(moves)]
    for copy in copies:
        copy.start()
    rows = held[0].shape[1]
    for number, (copy, ref) in enumerate(zip(copies, held)):
        copy.wait()
        for pair in range(H // 2):
            cols = rows_of(pair, LANES)
            packed[2 * pair, rows_of(number, rows)], packed[2 * pair + 1, rows_of(number, rows)] = (
                interleave(ref[0, :, cols], ref[1, :, cols])
            )
    copies[4].wait()
    copies[5].wait()
    row = lax.broadcasted_iota(jnp.int32, (INFO, LANES), 0)
    lane = lax.broadcasted_iota(jnp.int32, (INFO, LANES), 1)
    info = jnp.zeros((INFO, LANES), jnp.int32)
    for block in range(rows // BLK):
        for column in range(window_ref.shape[1]):
            at = block * BLK + (column // INFO) * SIZE
            here = (row == column % INFO) & (lane >= at) & (lane < at + BLK)
            info = jnp.where(here, window_ref[block, column], info)
    for frame in range(2):
        here = (row == INFO - 2 + frame) & (lane >= SIZE)
        info = jnp.where(here, lookback_ref[frame], info)
    info = info.astype(jnp.float32)
    for partner, ref in zip(order, out_refs):
        ref[: 4 * rows] = packed[place(partner, patch_count)]
        ref[4 * rows :] = info


def unpack_kernel(order, patch_count, *refs):
    in_refs, out_refs, packed = refs[:H], refs[H:-1], refs[-1]
    rows = out_refs[0].shape[1]
    for partner, ref in zip(order, in_refs):
        packed[place(partner, patch_count)] = ref[...]
    for pair in range(H // 2):
        cols = rows_of(pair, LANES)
        for number, ref in enumerate(out_refs):
            at = rows_of(number, rows)
            ref[0, :, cols], ref[1, :, cols] = interleave(
                packed[2 * pair, at], packed[2 * pair + 1, at]
            )


def visible_keys(frame):
    return range(max(0, frame - LOOK + 1), frame + 1)


def rows_of(index, count):
    return slice(index * count, (index + 1) * count)


def head_kernel(order, parts, columns, *refs):
    in_refs, out_refs = refs[:H], refs[H : 2 * H]
    held, done, qt, kt, vt, ct, tt, gt, gq, gk, gv, wts, bias = refs[2 * H :]
    rows = done.shape[1] // 4
    frames, _, patches = wts.shape
    pairs = frames // 2
    scale = 1.0 / math.sqrt(SIZE)

    for partner, ref in zip(order, in_refs):
        held[place(partner, parts)] = ref[...]

    def natural(number, pair):
        return held[rows_of(pair, parts), rows_of(number, rows)].reshape(patches, LANES)

    info = [held[part, 4 * rows : 4 * rows + INFO] for part in range(parts)]
    sides = [interleave(info[part], info[part + 1]) for part in range(0, parts, 2)]
    first = jnp.concatenate([side[0] for side in sides], axis=1)
    last = jnp.concatenate([side[1] for side in sides], axis=1)
    key_block = (lax.broadcasted_iota(jnp.int32, (patches, patches), 0) // BLK).astype(jnp.float32)
    seen = key_block == first[0:1]
    for column in range(1, columns):
        of = first if column < INFO else last
        seen = seen | (key_block == of[column % INFO : column % INFO + 1])
    bias[...] = jnp.where(seen, 0.0, -jnp.inf)

    for pair in range(pairs):
        at = rows_of(pair, LANES)
        qt[at] = natural(0, pair).T * scale
        kt[at] = natural(1, pair).T
        vt[at] = natural(2, pair).T
        ct[at] = natural(3, pair).T

    for frame in range(frames):
        tile = held[(frame // 2) * parts, 4 * rows : 4 * rows + INFO]
        _, tile = interleave(tile, tile)
        at = INFO - 2 + frame % 2
        lookback = tile[at : at + 1]
        for chunk in range(patches // LANES):
            cols = rows_of(chunk, LANES)
            query = qt[rows_of(frame, SIZE), cols]
            keys = visible_keys(frame)
            scores = []
            for key in keys:
                score = jnp.sum(query * kt[rows_of(key, SIZE), cols], axis=0, keepdims=True)
                scores.append(jnp.where(lookback > float(frame - key), score, -jnp.inf))
            top = scores[0]
            for score in scores[1:]:
                top = jnp.maximum(top, score)
            exps = [jnp.exp(score - top) for score in scores]
            total = exps[0]
            for term in exps[1:]:
                total = total + term
            value = jnp.zeros((SIZE, LANES), jnp.float32)
            for key, term in zip(keys, exps):
                weight = term / total
                wts[frame, frame - key : frame - key + 1, cols] = weight
                value = value + weight * vt[rows_of(key, SIZE), cols]
            tt[rows_of(frame, SIZE), cols] = value

    for pair in range(pairs):
        at = rows_of(pair, LANES)
        keys = natural(1, pair)
        high = keys.astype(jnp.bfloat16).astype(jnp.float32)
        low = keys - high
        mid = low.astype(jnp.bfloat16).astype(jnp.float32)
        upper = [x.astype(jnp.bfloat16) for x in interleave(high, mid)]
        lower = [x.astype(jnp.bfloat16) for x in interleave(high, low - mid)]
        value = tt[at].T
        high = value.astype(jnp.bfloat16).astype(jnp.float32)
        values = [x.astype(jnp.bfloat16) for x in interleave(high, value - high)]
        mixed = []
        for half in range(2):
            mine = rows_of(2 * pair + half, SIZE)
            query, grad = qt[mine], ct[mine]
            high, mid = split(query)
            low = query - high.astype(jnp.float32) - mid.astype(jnp.float32)
            low = low.astype(jnp.bfloat16)
            logits = dot(
                jnp.concatenate([upper[half]] * 2, axis=1),
                jnp.concatenate([high, high, mid, mid], axis=0),
                NN,
            )
            logits = logits + dot(lower[half], jnp.concatenate([low, high], axis=0), NN)
            logits = logits + bias[...]
            grad_weights = dot(jnp.concatenate([values[half]] * 2, axis=1), stacked(grad, 2), NN)
            top = jnp.max(logits, axis=0, keepdims=True)
            exps = jnp.exp(logits - top)
            share = 1.0 / jnp.sum(exps, axis=0, keepdims=True)
            high, low = split(exps)
            mix = heads_dot(tt[mine], high, low, NN) * share
            mixed.append(mix)
            gt[mine] = heads_dot(grad * share, high, low, NT)
            delta = jnp.sum(grad * mix, axis=0, keepdims=True)
            high, low = split(exps * (grad_weights - delta))
            gq[mine] = heads_dot(kt[mine], high, low, NN) * share
            gk[mine] = heads_dot(query * share, high, low, NT)
        mixed = jnp.concatenate(mixed, axis=0).T.reshape(parts, rows, LANES)
        done[rows_of(pair, parts), rows_of(0, rows)] = mixed

    gv[...] = jnp.zeros(gv.shape, jnp.float32)
    for frame in range(frames):
        mine = rows_of(frame, SIZE)
        for chunk in range(patches // LANES):
            cols = rows_of(chunk, LANES)
            query, grad = qt[mine, cols], gt[mine, cols]
            weights, terms = [], []
            inner = jnp.zeros((1, LANES), jnp.float32)
            for key in visible_keys(frame):
                weight = wts[frame, frame - key : frame - key + 1, cols]
                term = jnp.sum(grad * vt[rows_of(key, SIZE), cols], axis=0, keepdims=True)
                inner = inner + weight * term
                weights.append(weight)
                terms.append(term)
            grad_query = gq[mine, cols]
            for key, weight, term in zip(visible_keys(frame), weights, terms):
                of = rows_of(key, SIZE)
                score = weight * (term - inner)
                grad_query = grad_query + score * kt[of, cols]
                gk[of, cols] = gk[of, cols] + score * query
                gv[of, cols] = gv[of, cols] + weight * grad
            gq[mine, cols] = grad_query * scale

    for pair in range(pairs):
        at = rows_of(pair, LANES)
        for number, ref in enumerate((gq, gk, gv)):
            done[rows_of(pair, parts), rows_of(number + 1, rows)] = ref[at].T.reshape(
                parts, rows, LANES
            )
    for partner, ref in zip(order, out_refs):
        ref[...] = done[place(partner, parts)]


def exchange(blocks, order, patch_count):
    out = []
    for block, (frame, patch) in zip(blocks, order):
        pairs = [
            (i * patch_count + j, (i ^ frame) * patch_count + (j ^ patch))
            for i in range(H // patch_count)
            for j in range(patch_count)
        ]
        out.append(block if frame == patch == 0 else lax.ppermute(block, ("frame", "patch"), pairs))
    return out


def shards_by_head(queries, key_rows, value_rows, cotangent, lookback, window):
    frames_here, patches_here, model_width = queries.shape
    parts = lax.axis_size("patch")
    frames = frames_here * lax.axis_size("frame")
    patches = patches_here * parts
    order = partners(lax.axis_size("frame"), parts)
    vmem = pl.BlockSpec(memory_space=pltpu.VMEM)
    anywhere = pl.BlockSpec(memory_space=pl.ANY)

    def blocks(rows):
        return [jax.ShapeDtypeStruct((rows, LANES), jnp.float32)] * H

    def params(mebibytes):
        return pltpu.CompilerParams(vmem_limit_bytes=mebibytes * 1024 * 1024)

    packed = pl.pallas_call(
        lambda *refs: pack_kernel(order, parts, *refs),
        out_shape=blocks(4 * patches_here + INFO),
        in_specs=[anywhere] * 6,
        out_specs=[vmem] * H,
        scratch_shapes=[pltpu.VMEM(queries.shape, jnp.float32)] * 4
        + [
            pltpu.VMEM((H, 4 * patches_here, LANES), jnp.float32),
            pltpu.SMEM(window.shape, jnp.int32),
            pltpu.SMEM(lookback.shape, jnp.int32),
            pltpu.SemaphoreType.DMA((6,)),
        ],
        compiler_params=params(56),
        name="pack_heads",
    )(window, lookback, queries, key_rows, value_rows, cotangent)
    across = pltpu.VMEM((frames * SIZE, patches), jnp.float32)
    done = pl.pallas_call(
        lambda *refs: head_kernel(order, parts, window.shape[1], *refs),
        out_shape=blocks(4 * patches_here),
        in_specs=[vmem] * H,
        out_specs=[vmem] * H,
        scratch_shapes=[
            pltpu.VMEM((H, 4 * patches_here + INFO, LANES), jnp.float32),
            pltpu.VMEM((H, 4 * patches_here, LANES), jnp.float32),
        ]
        + [across] * 9
        + [
            pltpu.VMEM((frames, 8, patches), jnp.float32),
            pltpu.VMEM((patches, patches), jnp.float32),
        ],
        compiler_params=params(40),
        name="one_head",
    )(*exchange(packed, order, parts))
    return pl.pallas_call(
        lambda *refs: unpack_kernel(order, parts, *refs),
        out_shape=[jax.ShapeDtypeStruct(queries.shape, jnp.float32)] * 4,
        in_specs=[vmem] * H,
        out_specs=[vmem] * 4,
        scratch_shapes=[pltpu.VMEM((H, 4 * patches_here, LANES), jnp.float32)],
        compiler_params=params(40),
        name="unpack_heads",
    )(*exchange(done, order, parts))


def shards(queries, key_rows, value_rows, cotangent, lookback, window):
    frames_here, patches_here, model_width = queries.shape
    fits = (
        lax.axis_size("frame") * lax.axis_size("patch") == H
        and frames_here == 2
        and patches_here == SIZE
        and lax.axis_size("patch") in (2, 4, 8)
        and model_width == H * SIZE
    )
    form = shards_by_head if fits else shards_general
    return tuple(form(queries, key_rows, value_rows, cotangent, lookback, window))


def solution(mesh):
    rows = P(("traj", "frame"), "patch", None)
    return jax.shard_map(
        shards,
        mesh=mesh,
        in_specs=(rows, rows, rows, rows, P(("traj", "frame")), P(("traj", "patch"), None)),
        out_specs=(rows,) * 4,
        check_vma=False,
    )
```

```python
import math

import jax
import jax.numpy as jnp
from jax import lax
from jax.experimental import pallas as pl
from jax.experimental.pallas import tpu as pltpu
from jax.sharding import PartitionSpec as P

H = 16
BLK = 16
LOOK = 6
REACH = 6


def shifted(x, axis, by):
    count = lax.axis_size(axis)
    pairs = [(i, i + by) for i in range(count) if 0 <= i + by < count]
    return lax.ppermute(x, axis, pairs)


def passed_along(block, axis, distance):
    devices = range(lax.axis_size(axis))
    route = [((i - distance) % len(devices), i) for i in devices]
    return lax.ppermute(block, axis, route)


def split_heads(tensor, size_head):
    return tensor.reshape(tensor.shape[0], tensor.shape[1], H, size_head)


def shards_general(queries, key_rows, value_rows, cotangent, lookback, window):
    frames_here, patches_here, model_width = queries.shape
    size_head = model_width // H
    score_scale = 1.0 / math.sqrt(size_head)
    highest = lax.Precision.HIGHEST
    frame_index = lax.axis_index("frame")
    cycle_depth = (LOOK + frames_here - 2) // frames_here
    earlier = []
    carried = (key_rows, value_rows)
    for distance in range(cycle_depth):
        carried = shifted((carried[0], carried[1]), "frame", 1)
        earlier.append(carried)
    bank_keys = jnp.concatenate(
        [earlier[cycle_depth - 1 - number][0] for number in range(cycle_depth)] + [key_rows], axis=0
    )
    bank_values = jnp.concatenate(
        [earlier[cycle_depth - 1 - number][1] for number in range(cycle_depth)] + [value_rows],
        axis=0,
    )
    bank_frames = bank_keys.shape[0]
    q_heads = split_heads(queries, size_head)
    key_heads = split_heads(bank_keys, size_head)
    value_heads = split_heads(bank_values, size_head)
    query_frame = frame_index * frames_here + jnp.arange(frames_here, dtype=jnp.int32)
    key_frame = (frame_index - cycle_depth) * frames_here + jnp.arange(bank_frames, dtype=jnp.int32)
    offset = query_frame[:, None] - key_frame[None, :]
    visible = (offset >= 0) & (offset < lookback[:, None]) & (key_frame[None, :] >= 0)
    scores = jnp.einsum("fphe,jphe->phfj", q_heads, key_heads, precision=highest) * score_scale
    scores = jnp.where(visible, scores, -jnp.inf)
    weights = jax.nn.softmax(scores, axis=-1)
    temporal = jnp.einsum("phfj,jphe->fphe", weights, value_heads, precision=highest).reshape(
        frames_here, patches_here, model_width
    )
    patch_count = lax.axis_size("patch")
    patch_index = lax.axis_index("patch")
    blocks_here = patches_here // BLK
    reach_devices = -(-REACH // blocks_here)
    offsets = []
    for stride in range(-reach_devices, reach_devices + 1):
        if all(((stride - earlier_step) % patch_count != 0 for earlier_step in offsets)):
            offsets.append(stride)
    entries = []
    running_base = 0
    for stride in offsets:
        count_here = blocks_here if stride != 0 and abs(stride) == reach_devices else blocks_here
        first_block = 0 if stride >= 0 else blocks_here - count_here
        entries.append((stride, first_block, count_here, running_base))
        running_base = running_base + count_here
    count_slots = running_base
    near_banks = []
    for stride, first_block, count_here, base_slot in entries:
        rows_from = first_block * BLK
        rows_to = (first_block + count_here) * BLK
        piece = (key_rows, temporal)
        if stride == 0:
            near_banks.append(piece)
        else:
            near_banks.append(passed_along((piece[0], piece[1]), "patch", -stride))
    near_keys = jnp.concatenate([entry[0] for entry in near_banks], axis=1)
    near_values = jnp.concatenate([entry[1] for entry in near_banks], axis=1)
    owner_device = window // blocks_here
    relative = (owner_device - patch_index) % patch_count
    base_of = jnp.zeros(window.shape, jnp.int32)
    first_of = jnp.zeros(window.shape, jnp.int32)
    for stride, first_block, count_here, base_slot in entries:
        matches = relative == stride % patch_count
        base_of = jnp.where(matches, base_slot, base_of)
        first_of = jnp.where(matches, first_block, first_of)
    slot_index = base_of + window % blocks_here - first_of
    window_count = window.shape[1]
    key_blocks = near_keys.reshape(frames_here, count_slots, BLK, model_width)
    value_blocks = near_values.reshape(frames_here, count_slots, BLK, model_width)

    def frame_step(frame_items):
        query_part, key_part, value_part, grad_part = frame_items
        key_win = key_part[slot_index].reshape(blocks_here, window_count * BLK, H, size_head)
        value_win = value_part[slot_index].reshape(blocks_here, window_count * BLK, H, size_head)
        query_win = query_part.reshape(blocks_here, BLK, H, size_head)
        grad_win = grad_part.reshape(blocks_here, BLK, H, size_head)
        logits = jnp.einsum("bxhe,byhe->bhxy", query_win, key_win, precision=highest) * score_scale
        attention = jax.nn.softmax(logits, axis=-1)
        mixed_rows = jnp.einsum("bhxy,byhe->bxhe", attention, value_win, precision=highest)
        grad_attention = jnp.einsum("bxhe,byhe->bhxy", grad_win, value_win, precision=highest)
        grad_logits = attention * (
            grad_attention - jnp.sum(attention * grad_attention, axis=-1, keepdims=True)
        )
        grad_query = (
            jnp.einsum("bhxy,byhe->bxhe", grad_logits, key_win, precision=highest) * score_scale
        )
        grad_key = (
            jnp.einsum("bhxy,bxhe->byhe", grad_logits, query_win, precision=highest) * score_scale
        )
        grad_value = jnp.einsum("bhxy,bxhe->byhe", attention, grad_win, precision=highest)
        block_shape = (blocks_here, window_count, BLK, model_width)
        key_back = (
            jnp.zeros((count_slots, BLK, model_width), jnp.float32)
            .at[slot_index]
            .add(grad_key.reshape(block_shape))
        )
        value_back = (
            jnp.zeros((count_slots, BLK, model_width), jnp.float32)
            .at[slot_index]
            .add(grad_value.reshape(block_shape))
        )
        return (
            mixed_rows.reshape(patches_here, model_width),
            grad_query.reshape(patches_here, model_width),
            key_back,
            value_back,
        )

    mixed, grad_query_space, key_back, value_back = lax.map(
        frame_step, (queries, key_blocks, value_blocks, cotangent)
    )
    key_back = key_back.reshape(frames_here, count_slots * BLK, model_width)
    value_back = value_back.reshape(frames_here, count_slots * BLK, model_width)
    grad_key_space = jnp.zeros(queries.shape, jnp.float32)
    grad_temporal = jnp.zeros(queries.shape, jnp.float32)
    for stride, first_block, count_here, base_slot in entries:
        slot_from = base_slot * BLK
        slot_to = (base_slot + count_here) * BLK
        returned = (key_back[:, slot_from:slot_to], value_back[:, slot_from:slot_to])
        if stride != 0:
            returned = passed_along((returned[0], returned[1]), "patch", stride)
        rows_from = first_block * BLK
        rows_to = (first_block + count_here) * BLK
        grad_key_space = grad_key_space.at[:, rows_from:rows_to].add(returned[0])
        grad_temporal = grad_temporal.at[:, rows_from:rows_to].add(returned[1])
    grad_heads = split_heads(grad_temporal, size_head)
    grad_weights = jnp.einsum("fphe,jphe->phfj", grad_heads, value_heads, precision=highest)
    grad_scores = weights * (grad_weights - jnp.sum(weights * grad_weights, axis=-1, keepdims=True))
    grad_query_time = (
        jnp.einsum("phfj,jphe->fphe", grad_scores, key_heads, precision=highest) * score_scale
    )
    key_terms = (
        jnp.einsum("phfj,fphe->jphe", grad_scores, q_heads, precision=highest) * score_scale
    ).reshape(cycle_depth + 1, frames_here, patches_here, model_width)
    value_terms = jnp.einsum("phfj,fphe->jphe", weights, grad_heads, precision=highest).reshape(
        cycle_depth + 1, frames_here, patches_here, model_width
    )
    carried = (key_terms[0], value_terms[0])
    for distance in range(1, cycle_depth + 1):
        carried = shifted((carried[0], carried[1]), "frame", -1)
        carried = (carried[0] + key_terms[distance], carried[1] + value_terms[distance])
    grad_key_time, grad_value_time = carried
    grad_queries = grad_query_space + grad_query_time.reshape(
        frames_here, patches_here, model_width
    )
    grad_keys = grad_key_space + grad_key_time
    return (mixed, grad_queries, grad_keys, grad_value_time)


LANES = 128
SIZE = LANES // 2
INFO = 8
NN = ((1,), (0,))
NT = ((1,), (1,))


def interleave(first, second):
    axis = first.ndim - 1
    low = lax.broadcasted_iota(jnp.int32, first.shape, axis) < SIZE
    return (
        jnp.where(low, first, pltpu.roll(second, SIZE, axis)),
        jnp.where(low, pltpu.roll(first, SIZE, axis), second),
    )


def dot(a, b, dims):
    return lax.dot_general(a, b, (dims, ((), ())), preferred_element_type=jnp.float32)


def split(x):
    high = x.astype(jnp.bfloat16)
    return high, (x - high.astype(jnp.float32)).astype(jnp.bfloat16)


def stacked(x, times):
    high, low = split(x)
    return jnp.concatenate([high] * times + [low] * times, axis=0)


def heads_dot(x, high, low, dims):
    both = stacked(x, 1)
    out = dot(both, high, dims)
    return out[:SIZE] + (out[SIZE:] + dot(both[:SIZE], low, dims))


def partners(frame_count, patch_count):
    every = [(frame, patch) for frame in range(frame_count) for patch in range(patch_count)]
    far = [at for at in every if at[1] >= patch_count // 2]
    near = [at for at in every[1:] if at[1] < patch_count // 2]
    order = every[:1] + far[:1]
    for number, at in enumerate(far[1:]):
        share = slice(number * len(near) // len(far[1:]), (number + 1) * len(near) // len(far[1:]))
        order += near[share] + [at] if number else [at] + near[share]
    return order


def place(partner, patch_count):
    return (
        lax.bitwise_xor(lax.axis_index("frame"), partner[0]),
        lax.bitwise_xor(lax.axis_index("patch"), partner[1]),
    )


def low_lanes(rows):
    return lax.broadcasted_iota(jnp.int32, (rows, LANES), 1) < SIZE


def head_columns(head):
    return pl.ds(pl.multiple_of(head // 2 * LANES, LANES), LANES)


def pack_kernel(order, patch_count, window, lookback, *refs):
    arrays, out_refs = refs[:4], refs[4 : 4 + H]
    held, (window_ref, lookback_ref, sems) = refs[4 + H : 8 + H], refs[8 + H :]
    moves = list(zip((window, lookback, *arrays), (window_ref, lookback_ref, *held)))
    copies = [pltpu.make_async_copy(a, b, sems.at[n]) for n, (a, b) in enumerate(moves)]
    for copy in copies:
        copy.start()
    copies[0].wait()
    copies[1].wait()
    rows = held[0].shape[1]
    row = lax.broadcasted_iota(jnp.int32, (INFO, LANES), 0)
    lane = lax.broadcasted_iota(jnp.int32, (INFO, LANES), 1)
    info = jnp.zeros((INFO, LANES), jnp.int32)
    for block in range(rows // BLK):
        for column in range(window_ref.shape[1]):
            at = block * BLK + (column // INFO) * SIZE
            here = (row == column % INFO) & (lane >= at) & (lane < at + BLK)
            info = jnp.where(here, window_ref[block, column], info)
    for frame in range(2):
        here = (row == INFO - 2 + frame) & (lane >= SIZE)
        info = jnp.where(here, lookback_ref[frame], info)
    info = info.astype(jnp.float32)
    for ref in out_refs:
        if ref.shape[0] > 4 * rows:
            ref[4 * rows :] = info
    low = low_lanes(rows).astype(jnp.int32)
    for number, (copy, ref) in enumerate(zip(copies[2:], held)):
        copy.wait()
        for partner, out_ref in zip(order, out_refs):
            frame, patch = place(partner, patch_count)
            head = frame * patch_count + patch
            odd = head % 2
            cols = head_columns(head)
            kept, moved = ref[odd, :, cols], ref[1 - odd, :, cols]
            out_ref[rows_of(number, rows)] = jnp.where(
                low != odd, kept, pltpu.roll(moved, SIZE, 1)
            )


def unpack_kernel(order, patch_count, *refs):
    in_refs, out_refs, held, sems = refs[:H], refs[H : H + 4], refs[H + 4 : H + 8], refs[H + 8]
    rows = held[0].shape[1]
    low = low_lanes(rows)
    copies = []
    for number, ref in enumerate(held):
        at = rows_of(number, rows)
        for (frame, patch), in_ref in zip(order, in_refs):
            if patch % 2:
                continue
            other = in_refs[order.index((frame, patch + 1))]
            frame, patch = place((frame, patch), patch_count)
            head = frame * patch_count + patch
            odd = jnp.full((rows, LANES), head % 2, jnp.int32) == 1
            here, there = in_ref[at], other[at]
            first, second = interleave(jnp.where(odd, there, here), jnp.where(odd, here, there))
            cols = head_columns(head)
            ref[0, :, cols] = first
            ref[1, :, cols] = second
        copies.append(pltpu.make_async_copy(ref, out_refs[number], sems.at[number]))
        copies[-1].start()
    for copy in copies:
        copy.wait()


def visible_keys(frame):
    return range(max(0, frame - LOOK + 1), frame + 1)


def rows_of(index, count):
    return slice(index * count, (index + 1) * count)


def head_kernel(order, parts, columns, *refs):
    in_refs, out_refs = refs[:H], refs[H : 2 * H]
    held, done, windows, lookbacks = refs[2 * H : 2 * H + 4]
    qt, kt, vt, ct, tt, gt, gq, gk, gv, wts, bias, sem = refs[2 * H + 4 :]
    rows = done.shape[1] // 4
    frames, _, patches = wts.shape
    pairs = frames // 2
    scale = 1.0 / math.sqrt(SIZE)

    own = place(order[0], parts)
    own = pltpu.make_async_copy(in_refs[0], held.at[own[0] * parts + own[1]], sem)
    own.start()
    for partner, ref in zip(order[1:], in_refs[1:]):
        frame, patch = place(partner, parts)
        held[frame * parts + patch, : 4 * rows] = ref[: 4 * rows]
        if partner[0] == 0:
            windows[patch] = ref[4 * rows :]
        if partner[1] == 0:
            lookbacks[frame] = ref[4 * rows :]
    own.wait()
    frame, patch = place(order[0], parts)
    windows[patch] = held[frame * parts + patch, 4 * rows :]
    lookbacks[frame] = held[frame * parts + patch, 4 * rows :]

    def natural(number, pair):
        return held[rows_of(pair, parts), rows_of(number, rows)].reshape(patches, LANES)

    sides = [interleave(windows[part], windows[part + 1]) for part in range(0, parts, 2)]
    first = jnp.concatenate([side[0] for side in sides], axis=1)
    last = jnp.concatenate([side[1] for side in sides], axis=1)
    key_block = (lax.broadcasted_iota(jnp.int32, (patches, patches), 0) // BLK).astype(jnp.float32)
    seen = key_block == first[0:1]
    for column in range(1, columns):
        of = first if column < INFO else last
        seen = seen | (key_block == of[column % INFO : column % INFO + 1])
    bias[...] = jnp.where(seen, 0.0, -jnp.inf)

    for pair in range(pairs):
        at = rows_of(pair, LANES)
        qt[at] = natural(0, pair).T * scale
        kt[at] = natural(1, pair).T
        vt[at] = natural(2, pair).T
        ct[at] = natural(3, pair).T

    for frame in range(frames):
        _, tile = interleave(lookbacks[frame // 2], lookbacks[frame // 2])
        at = INFO - 2 + frame % 2
        lookback = tile[at : at + 1]
        for chunk in range(patches // LANES):
            cols = rows_of(chunk, LANES)
            query = qt[rows_of(frame, SIZE), cols]
            keys = visible_keys(frame)
            scores = []
            for key in keys:
                score = jnp.sum(query * kt[rows_of(key, SIZE), cols], axis=0, keepdims=True)
                scores.append(jnp.where(lookback > float(frame - key), score, -jnp.inf))
            top = scores[0]
            for score in scores[1:]:
                top = jnp.maximum(top, score)
            exps = [jnp.exp(score - top) for score in scores]
            total = exps[0]
            for term in exps[1:]:
                total = total + term
            value = jnp.zeros((SIZE, LANES), jnp.float32)
            for key, term in zip(keys, exps):
                weight = term / total
                wts[frame, frame - key : frame - key + 1, cols] = weight
                value = value + weight * vt[rows_of(key, SIZE), cols]
            tt[rows_of(frame, SIZE), cols] = value

    for pair in range(pairs):
        at = rows_of(pair, LANES)
        keys = natural(1, pair)
        high = keys.astype(jnp.bfloat16).astype(jnp.float32)
        low = keys - high
        mid = low.astype(jnp.bfloat16).astype(jnp.float32)
        upper = [x.astype(jnp.bfloat16) for x in interleave(high, mid)]
        lower = [x.astype(jnp.bfloat16) for x in interleave(high, low - mid)]
        value = tt[at].T
        high = value.astype(jnp.bfloat16).astype(jnp.float32)
        values = [x.astype(jnp.bfloat16) for x in interleave(high, value - high)]
        mixed = []
        for half in range(2):
            mine = rows_of(2 * pair + half, SIZE)
            query, grad = qt[mine], ct[mine]
            high, mid = split(query)
            low = query - high.astype(jnp.float32) - mid.astype(jnp.float32)
            low = low.astype(jnp.bfloat16)
            logits = dot(
                jnp.concatenate([upper[half]] * 2, axis=1),
                jnp.concatenate([high, high, mid, mid], axis=0),
                NN,
            )
            logits = logits + dot(lower[half], jnp.concatenate([low, high], axis=0), NN)
            logits = logits + bias[...]
            grad_weights = dot(jnp.concatenate([values[half]] * 2, axis=1), stacked(grad, 2), NN)
            top = jnp.max(logits, axis=0, keepdims=True)
            exps = jnp.exp(logits - top)
            share = 1.0 / jnp.sum(exps, axis=0, keepdims=True)
            high, low = split(exps)
            mix = heads_dot(tt[mine], high, low, NN) * share
            mixed.append(mix)
            gt[mine] = heads_dot(grad * share, high, low, NT)
            delta = jnp.sum(grad * mix, axis=0, keepdims=True)
            high, low = split(exps * (grad_weights - delta))
            gq[mine] = heads_dot(kt[mine], high, low, NN) * share
            gk[mine] = heads_dot(query * share, high, low, NT)
        mixed = jnp.concatenate(mixed, axis=0).T.reshape(parts, rows, LANES)
        done[rows_of(pair, parts), rows_of(0, rows)] = mixed

    gv[...] = jnp.zeros(gv.shape, jnp.float32)
    for frame in range(frames):
        mine = rows_of(frame, SIZE)
        for chunk in range(patches // LANES):
            cols = rows_of(chunk, LANES)
            query, grad = qt[mine, cols], gt[mine, cols]
            weights, terms = [], []
            inner = jnp.zeros((1, LANES), jnp.float32)
            for key in visible_keys(frame):
                weight = wts[frame, frame - key : frame - key + 1, cols]
                term = jnp.sum(grad * vt[rows_of(key, SIZE), cols], axis=0, keepdims=True)
                inner = inner + weight * term
                weights.append(weight)
                terms.append(term)
            grad_query = gq[mine, cols]
            for key, weight, term in zip(visible_keys(frame), weights, terms):
                of = rows_of(key, SIZE)
                score = weight * (term - inner)
                grad_query = grad_query + score * kt[of, cols]
                gk[of, cols] = gk[of, cols] + score * query
                gv[of, cols] = gv[of, cols] + weight * grad
            gq[mine, cols] = grad_query * scale

    for pair in range(pairs):
        at = rows_of(pair, LANES)
        for number, ref in enumerate((gq, gk, gv)):
            done[rows_of(pair, parts), rows_of(number + 1, rows)] = ref[at].T.reshape(
                parts, rows, LANES
            )
    for partner, ref in zip(order, out_refs):
        frame, patch = place(partner, parts)
        ref[...] = done[frame * parts + patch]


def exchange(blocks, order, patch_count):
    out = []
    for block, (frame, patch) in zip(blocks, order):
        pairs = [
            (i * patch_count + j, (i ^ frame) * patch_count + (j ^ patch))
            for i in range(H // patch_count)
            for j in range(patch_count)
        ]
        out.append(block if frame == patch == 0 else lax.ppermute(block, ("frame", "patch"), pairs))
    return out


def shards_by_head(queries, key_rows, value_rows, cotangent, lookback, window):
    frames_here, patches_here, model_width = queries.shape
    parts = lax.axis_size("patch")
    frames = frames_here * lax.axis_size("frame")
    patches = patches_here * parts
    order = partners(lax.axis_size("frame"), parts)
    vmem = pl.BlockSpec(memory_space=pltpu.VMEM)
    anywhere = pl.BlockSpec(memory_space=pl.ANY)

    def blocks(info):
        return [
            jax.ShapeDtypeStruct((4 * patches_here + info, LANES), jnp.float32)
            for _ in order
        ]

    def params(mebibytes):
        return pltpu.CompilerParams(vmem_limit_bytes=mebibytes * 1024 * 1024)

    packed = pl.pallas_call(
        lambda *refs: pack_kernel(order, parts, *refs),
        out_shape=blocks(INFO),
        in_specs=[anywhere] * 6,
        out_specs=[vmem] * H,
        scratch_shapes=[pltpu.VMEM(queries.shape, jnp.float32)] * 4
        + [
            pltpu.SMEM(window.shape, jnp.int32),
            pltpu.SMEM(lookback.shape, jnp.int32),
            pltpu.SemaphoreType.DMA((6,)),
        ],
        compiler_params=params(56),
        name="pack_heads",
    )(window, lookback, queries, key_rows, value_rows, cotangent)
    across = pltpu.VMEM((frames * SIZE, patches), jnp.float32)
    done = pl.pallas_call(
        lambda *refs: head_kernel(order, parts, window.shape[1], *refs),
        out_shape=blocks(0),
        in_specs=[anywhere] + [vmem] * (H - 1),
        out_specs=[vmem] * H,
        scratch_shapes=[
            pltpu.VMEM((H, 4 * patches_here + INFO, LANES), jnp.float32),
            pltpu.VMEM((H, 4 * patches_here, LANES), jnp.float32),
            pltpu.VMEM((parts, INFO, LANES), jnp.float32),
            pltpu.VMEM((H // parts, INFO, LANES), jnp.float32),
        ]
        + [across] * 9
        + [
            pltpu.VMEM((frames, 8, patches), jnp.float32),
            pltpu.VMEM((patches, patches), jnp.float32),
            pltpu.SemaphoreType.DMA,
        ],
        compiler_params=params(40),
        name="one_head",
    )(*exchange(packed, order, parts))
    return pl.pallas_call(
        lambda *refs: unpack_kernel(order, parts, *refs),
        out_shape=[jax.ShapeDtypeStruct(queries.shape, jnp.float32)] * 4,
        in_specs=[vmem] * H,
        out_specs=[anywhere] * 4,
        scratch_shapes=[pltpu.VMEM(queries.shape, jnp.float32)] * 4
        + [pltpu.SemaphoreType.DMA((4,))],
        compiler_params=params(40),
        name="unpack_heads",
    )(*exchange(done, order, parts))


def shards(queries, key_rows, value_rows, cotangent, lookback, window):
    frames_here, patches_here, model_width = queries.shape
    fits = (
        lax.axis_size("frame") * lax.axis_size("patch") == H
        and frames_here == 2
        and patches_here == SIZE
        and lax.axis_size("patch") in (2, 4, 8)
        and model_width == H * SIZE
    )
    form = shards_by_head if fits else shards_general
    return tuple(form(queries, key_rows, value_rows, cotangent, lookback, window))


def solution(mesh):
    rows = P(("traj", "frame"), "patch", None)
    return jax.shard_map(
        shards,
        mesh=mesh,
        in_specs=(rows, rows, rows, rows, P(("traj", "frame")), P(("traj", "patch"), None)),
        out_specs=(rows,) * 4,
        check_vma=False,
    )
```

```python
import math

import jax
import jax.numpy as jnp
from jax import lax
from jax.experimental import pallas as pl
from jax.experimental.pallas import tpu as pltpu
from jax.sharding import PartitionSpec as P

H = 16
BLK = 16
LOOK = 6
REACH = 6


def shifted(x, axis, by):
    count = lax.axis_size(axis)
    pairs = [(i, i + by) for i in range(count) if 0 <= i + by < count]
    return lax.ppermute(x, axis, pairs)


def passed_along(block, axis, distance):
    devices = range(lax.axis_size(axis))
    route = [((i - distance) % len(devices), i) for i in devices]
    return lax.ppermute(block, axis, route)


def split_heads(tensor, size_head):
    return tensor.reshape(tensor.shape[0], tensor.shape[1], H, size_head)


def shards_general(queries, key_rows, value_rows, cotangent, lookback, window):
    frames_here, patches_here, model_width = queries.shape
    size_head = model_width // H
    score_scale = 1.0 / math.sqrt(size_head)
    highest = lax.Precision.HIGHEST
    frame_index = lax.axis_index("frame")
    cycle_depth = (LOOK + frames_here - 2) // frames_here
    earlier = []
    carried = (key_rows, value_rows)
    for distance in range(cycle_depth):
        carried = shifted((carried[0], carried[1]), "frame", 1)
        earlier.append(carried)
    bank_keys = jnp.concatenate(
        [earlier[cycle_depth - 1 - number][0] for number in range(cycle_depth)] + [key_rows], axis=0
    )
    bank_values = jnp.concatenate(
        [earlier[cycle_depth - 1 - number][1] for number in range(cycle_depth)] + [value_rows],
        axis=0,
    )
    bank_frames = bank_keys.shape[0]
    q_heads = split_heads(queries, size_head)
    key_heads = split_heads(bank_keys, size_head)
    value_heads = split_heads(bank_values, size_head)
    query_frame = frame_index * frames_here + jnp.arange(frames_here, dtype=jnp.int32)
    key_frame = (frame_index - cycle_depth) * frames_here + jnp.arange(bank_frames, dtype=jnp.int32)
    offset = query_frame[:, None] - key_frame[None, :]
    visible = (offset >= 0) & (offset < lookback[:, None]) & (key_frame[None, :] >= 0)
    scores = jnp.einsum("fphe,jphe->phfj", q_heads, key_heads, precision=highest) * score_scale
    scores = jnp.where(visible, scores, -jnp.inf)
    weights = jax.nn.softmax(scores, axis=-1)
    temporal = jnp.einsum("phfj,jphe->fphe", weights, value_heads, precision=highest).reshape(
        frames_here, patches_here, model_width
    )
    patch_count = lax.axis_size("patch")
    patch_index = lax.axis_index("patch")
    blocks_here = patches_here // BLK
    reach_devices = -(-REACH // blocks_here)
    offsets = []
    for stride in range(-reach_devices, reach_devices + 1):
        if all(((stride - earlier_step) % patch_count != 0 for earlier_step in offsets)):
            offsets.append(stride)
    entries = []
    running_base = 0
    for stride in offsets:
        count_here = blocks_here if stride != 0 and abs(stride) == reach_devices else blocks_here
        first_block = 0 if stride >= 0 else blocks_here - count_here
        entries.append((stride, first_block, count_here, running_base))
        running_base = running_base + count_here
    count_slots = running_base
    near_banks = []
    for stride, first_block, count_here, base_slot in entries:
        rows_from = first_block * BLK
        rows_to = (first_block + count_here) * BLK
        piece = (key_rows, temporal)
        if stride == 0:
            near_banks.append(piece)
        else:
            near_banks.append(passed_along((piece[0], piece[1]), "patch", -stride))
    near_keys = jnp.concatenate([entry[0] for entry in near_banks], axis=1)
    near_values = jnp.concatenate([entry[1] for entry in near_banks], axis=1)
    owner_device = window // blocks_here
    relative = (owner_device - patch_index) % patch_count
    base_of = jnp.zeros(window.shape, jnp.int32)
    first_of = jnp.zeros(window.shape, jnp.int32)
    for stride, first_block, count_here, base_slot in entries:
        matches = relative == stride % patch_count
        base_of = jnp.where(matches, base_slot, base_of)
        first_of = jnp.where(matches, first_block, first_of)
    slot_index = base_of + window % blocks_here - first_of
    window_count = window.shape[1]
    key_blocks = near_keys.reshape(frames_here, count_slots, BLK, model_width)
    value_blocks = near_values.reshape(frames_here, count_slots, BLK, model_width)

    def frame_step(frame_items):
        query_part, key_part, value_part, grad_part = frame_items
        key_win = key_part[slot_index].reshape(blocks_here, window_count * BLK, H, size_head)
        value_win = value_part[slot_index].reshape(blocks_here, window_count * BLK, H, size_head)
        query_win = query_part.reshape(blocks_here, BLK, H, size_head)
        grad_win = grad_part.reshape(blocks_here, BLK, H, size_head)
        logits = jnp.einsum("bxhe,byhe->bhxy", query_win, key_win, precision=highest) * score_scale
        attention = jax.nn.softmax(logits, axis=-1)
        mixed_rows = jnp.einsum("bhxy,byhe->bxhe", attention, value_win, precision=highest)
        grad_attention = jnp.einsum("bxhe,byhe->bhxy", grad_win, value_win, precision=highest)
        grad_logits = attention * (
            grad_attention - jnp.sum(attention * grad_attention, axis=-1, keepdims=True)
        )
        grad_query = (
            jnp.einsum("bhxy,byhe->bxhe", grad_logits, key_win, precision=highest) * score_scale
        )
        grad_key = (
            jnp.einsum("bhxy,bxhe->byhe", grad_logits, query_win, precision=highest) * score_scale
        )
        grad_value = jnp.einsum("bhxy,bxhe->byhe", attention, grad_win, precision=highest)
        block_shape = (blocks_here, window_count, BLK, model_width)
        key_back = (
            jnp.zeros((count_slots, BLK, model_width), jnp.float32)
            .at[slot_index]
            .add(grad_key.reshape(block_shape))
        )
        value_back = (
            jnp.zeros((count_slots, BLK, model_width), jnp.float32)
            .at[slot_index]
            .add(grad_value.reshape(block_shape))
        )
        return (
            mixed_rows.reshape(patches_here, model_width),
            grad_query.reshape(patches_here, model_width),
            key_back,
            value_back,
        )

    mixed, grad_query_space, key_back, value_back = lax.map(
        frame_step, (queries, key_blocks, value_blocks, cotangent)
    )
    key_back = key_back.reshape(frames_here, count_slots * BLK, model_width)
    value_back = value_back.reshape(frames_here, count_slots * BLK, model_width)
    grad_key_space = jnp.zeros(queries.shape, jnp.float32)
    grad_temporal = jnp.zeros(queries.shape, jnp.float32)
    for stride, first_block, count_here, base_slot in entries:
        slot_from = base_slot * BLK
        slot_to = (base_slot + count_here) * BLK
        returned = (key_back[:, slot_from:slot_to], value_back[:, slot_from:slot_to])
        if stride != 0:
            returned = passed_along((returned[0], returned[1]), "patch", stride)
        rows_from = first_block * BLK
        rows_to = (first_block + count_here) * BLK
        grad_key_space = grad_key_space.at[:, rows_from:rows_to].add(returned[0])
        grad_temporal = grad_temporal.at[:, rows_from:rows_to].add(returned[1])
    grad_heads = split_heads(grad_temporal, size_head)
    grad_weights = jnp.einsum("fphe,jphe->phfj", grad_heads, value_heads, precision=highest)
    grad_scores = weights * (grad_weights - jnp.sum(weights * grad_weights, axis=-1, keepdims=True))
    grad_query_time = (
        jnp.einsum("phfj,jphe->fphe", grad_scores, key_heads, precision=highest) * score_scale
    )
    key_terms = (
        jnp.einsum("phfj,fphe->jphe", grad_scores, q_heads, precision=highest) * score_scale
    ).reshape(cycle_depth + 1, frames_here, patches_here, model_width)
    value_terms = jnp.einsum("phfj,fphe->jphe", weights, grad_heads, precision=highest).reshape(
        cycle_depth + 1, frames_here, patches_here, model_width
    )
    carried = (key_terms[0], value_terms[0])
    for distance in range(1, cycle_depth + 1):
        carried = shifted((carried[0], carried[1]), "frame", -1)
        carried = (carried[0] + key_terms[distance], carried[1] + value_terms[distance])
    grad_key_time, grad_value_time = carried
    grad_queries = grad_query_space + grad_query_time.reshape(
        frames_here, patches_here, model_width
    )
    grad_keys = grad_key_space + grad_key_time
    return (mixed, grad_queries, grad_keys, grad_value_time)


LANES = 128
SIZE = LANES // 2
INFO = 8
OUTWARD = (
    (0, 0), (3, 3), (0, 1), (1, 0), (1, 2), (1, 1), (1, 3), (2, 2),
    (2, 1), (2, 3), (3, 0), (3, 2), (3, 1), (0, 2), (2, 0), (0, 3),
)
HOMEWARD = (
    (0, 0), (3, 3), (0, 1), (1, 0), (1, 2), (1, 1), (1, 3), (2, 2),
    (2, 1), (2, 3), (3, 0), (3, 2), (3, 1), (0, 2), (2, 0), (0, 3),
)
NN = ((1,), (0,))
NT = ((1,), (1,))


def interleave(first, second):
    axis = first.ndim - 1
    low = lax.broadcasted_iota(jnp.int32, first.shape, axis) < SIZE
    return (
        jnp.where(low, first, pltpu.roll(second, SIZE, axis)),
        jnp.where(low, pltpu.roll(first, SIZE, axis), second),
    )


def dot(a, b, dims):
    return lax.dot_general(a, b, (dims, ((), ())), preferred_element_type=jnp.float32)


def split(x):
    high = x.astype(jnp.bfloat16)
    return high, (x - high.astype(jnp.float32)).astype(jnp.bfloat16)


def stacked(x, times):
    high, low = split(x)
    return jnp.concatenate([high] * times + [low] * times, axis=0)


def heads_dot(x, high, low, dims):
    both = stacked(x, 1)
    out = dot(both, high, dims)
    return out[:SIZE] + (out[SIZE:] + dot(both[:SIZE], low, dims))


def place(partner, patch_count):
    frame = lax.bitwise_xor(lax.axis_index("frame"), partner[0])
    return frame * patch_count + lax.bitwise_xor(lax.axis_index("patch"), partner[1])


def columns_of(head):
    return pl.ds(pl.multiple_of(head // 2 * LANES, LANES), LANES)


def low_lanes(rows):
    return lax.broadcasted_iota(jnp.int32, (rows, LANES), 1) < SIZE


def side_by_side(ref, head, cols):
    odd = head % 2
    kept, moved = ref[odd, :, cols], ref[1 - odd, :, cols]
    low = low_lanes(kept.shape[0]).astype(jnp.int32)
    return jnp.where(low != odd, kept, pltpu.roll(moved, SIZE, 1))


def whole_numbers(window, lookback, rows):
    row = lax.broadcasted_iota(jnp.int32, (INFO, LANES), 0)
    lane = lax.broadcasted_iota(jnp.int32, (INFO, LANES), 1)
    info = jnp.zeros((INFO, LANES), jnp.int32)
    for block in range(rows // BLK):
        for column in range(window.shape[1]):
            at = block * BLK + (column // INFO) * SIZE
            here = (row == column % INFO) & (lane >= at) & (lane < at + BLK)
            info = jnp.where(here, window[block, column], info)
    for frame in range(2):
        here = (row == INFO - 2 + frame) & (lane >= SIZE)
        info = jnp.where(here, lookback[frame], info)
    return info.astype(jnp.float32)


def fetch(moves, sems):
    copies = [pltpu.make_async_copy(a, b, sems.at[n]) for n, (a, b) in enumerate(moves)]
    for copy in copies:
        copy.start()
    return copies


def pack_kernel(order, parts, window, lookback, *refs):
    arrays, out_refs = refs[:4], refs[4 : 3 + H]
    held, window_ref, lookback_ref, sems = refs[3 + H : 7 + H], *refs[7 + H :]
    moves = [(window, window_ref), (lookback, lookback_ref)]
    moves += [(a.at[frame], b.at[frame]) for a, b in zip(arrays, held) for frame in range(2)]
    copies = fetch(moves, sems)
    copies[0].wait()
    copies[1].wait()
    rows = held[0].shape[1]
    info = whole_numbers(window_ref, lookback_ref, rows)
    for ref in out_refs:
        ref[4 * rows :] = info
    for number, ref in enumerate(held):
        copies[2 + 2 * number].wait()
        copies[3 + 2 * number].wait()
        for partner, out_ref in zip(order, out_refs):
            head = place(partner, parts)
            out_ref[rows_of(number, rows)] = side_by_side(ref, head, columns_of(head))


def unpack_kernel(order, groups, parts, *refs):
    in_refs, out_refs, held, sems = refs[:H], refs[H : H + 4], refs[H + 4 : H + 8], refs[H + 8]
    rows = held[0].shape[1]
    copies = []
    for number, ref in enumerate(held):
        at = rows_of(number, rows)
        for frame in range(groups):
            for patch in range(0, parts, 2):
                head = place((frame, patch), parts)
                odd = jnp.full((rows, LANES), head % 2, jnp.int32) == 1
                here = in_refs[order.index((frame, patch))][at]
                there = in_refs[order.index((frame, patch + 1))][at]
                first, second = interleave(jnp.where(odd, there, here), jnp.where(odd, here, there))
                cols = columns_of(head)
                ref[0, :, cols] = first
                ref[1, :, cols] = second
        copies.append(pltpu.make_async_copy(ref, out_refs[number], sems.at[number]))
        copies[-1].start()
    for copy in copies:
        copy.wait()


def visible_keys(frame):
    return range(max(0, frame - LOOK + 1), frame + 1)


def rows_of(index, count):
    return slice(index * count, (index + 1) * count)


def head_kernel(order, back, groups, parts, window, lookback, *refs):
    arrays, in_refs, out_refs = refs[:4], refs[4 : 3 + H], refs[3 + H : 3 + 2 * H]
    held, own_ref, window_ref, lookback_ref, lookbacks, sems = refs[3 + 2 * H : 12 + 2 * H][:4], *refs[
        7 + 2 * H : 12 + 2 * H
    ]
    qt, kt, vt, ct, tt, mt, gt, gq, gk, gv, wts, bias = refs[12 + 2 * H :]
    rows = own_ref.shape[0] // 4
    frames, _, patches = wts.shape
    scale = 1.0 / math.sqrt(SIZE)

    head = place((0, 0), parts)
    moves = [(window, window_ref), (lookback, lookback_ref)]
    moves += [(a.at[:, :, columns_of(head)], b) for a, b in zip(arrays, held)]
    copies = fetch(moves, sems)

    def natural(number, group):
        at = rows_of(number, rows)
        found = [in_refs[order.index((group, part)) - 1][at] if group or part else own_ref[at] for part in range(parts)]
        return jnp.concatenate(found, axis=0)

    def tile(group, part):
        return in_refs[order.index((group, part)) - 1][4 * rows :] if group or part else info

    def pair_rows(group):
        at = lax.bitwise_xor(lax.axis_index("frame"), group) * LANES
        return pl.ds(pl.multiple_of(at, LANES), LANES)

    def turn(group):
        at = pair_rows(group)
        qt[at] = natural(0, group).T * scale
        kt[at] = natural(1, group).T
        vt[at] = natural(2, group).T
        ct[at] = natural(3, group).T
        lookbacks[lax.bitwise_xor(lax.axis_index("frame"), group)] = tile(group, 0)

    for group in range(1, groups):
        turn(group)
    for copy in copies:
        copy.wait()
    for number, ref in enumerate(held):
        own_ref[rows_of(number, rows)] = side_by_side(ref, head, slice(None))
    info = whole_numbers(window_ref, lookback_ref, rows)
    turn(0)

    sides = [interleave(tile(0, part), tile(0, part + 1)) for part in range(0, parts, 2)]
    first = jnp.concatenate([side[0] for side in sides], axis=1)
    last = jnp.concatenate([side[1] for side in sides], axis=1)
    count = rows // BLK
    block = lax.broadcasted_iota(jnp.int32, (parts * count, patches), 0)
    block = lax.bitwise_xor(block // count, lax.axis_index("patch")) * count + block % count
    block = block.astype(jnp.float32)
    seen = block == first[0:1]
    for column in range(1, window.shape[1]):
        of = first if column < INFO else last
        seen = seen | (block == of[column % INFO : column % INFO + 1])
    mask = jnp.where(seen, 0.0, -jnp.inf)
    for number in range(parts * count):
        bias[rows_of(number, BLK)] = jnp.broadcast_to(mask[number : number + 1], (BLK, patches))

    for frame in range(frames):
        _, given = interleave(lookbacks[frame // 2], lookbacks[frame // 2])
        at = INFO - 2 + frame % 2
        seen_frames = given[at : at + 1]
        for chunk in range(patches // LANES):
            cols = rows_of(chunk, LANES)
            query = qt[rows_of(frame, SIZE), cols]
            keys = visible_keys(frame)
            scores = []
            for key in keys:
                score = jnp.sum(query * kt[rows_of(key, SIZE), cols], axis=0, keepdims=True)
                scores.append(jnp.where(seen_frames > float(frame - key), score, -jnp.inf))
            top = scores[0]
            for score in scores[1:]:
                top = jnp.maximum(top, score)
            exps = [jnp.exp(score - top) for score in scores]
            total = exps[0]
            for term in exps[1:]:
                total = total + term
            value = jnp.zeros((SIZE, LANES), jnp.float32)
            for key, term in zip(keys, exps):
                weight = term / total
                wts[frame, frame - key : frame - key + 1, cols] = weight
                value = value + weight * vt[rows_of(key, SIZE), cols]
            tt[rows_of(frame, SIZE), cols] = value

    for pair in range(frames // 2):
        at = rows_of(pair, LANES)
        keys = kt[at].T
        high = keys.astype(jnp.bfloat16).astype(jnp.float32)
        low = keys - high
        mid = low.astype(jnp.bfloat16).astype(jnp.float32)
        upper = [x.astype(jnp.bfloat16) for x in interleave(high, mid)]
        lower = [x.astype(jnp.bfloat16) for x in interleave(high, low - mid)]
        value = tt[at].T
        high = value.astype(jnp.bfloat16).astype(jnp.float32)
        values = [x.astype(jnp.bfloat16) for x in interleave(high, value - high)]
        for half in range(2):
            mine = rows_of(2 * pair + half, SIZE)
            query, grad = qt[mine], ct[mine]
            high, mid = split(query)
            low = query - high.astype(jnp.float32) - mid.astype(jnp.float32)
            low = low.astype(jnp.bfloat16)
            logits = dot(
                jnp.concatenate([upper[half]] * 2, axis=1),
                jnp.concatenate([high, high, mid, mid], axis=0),
                NN,
            )
            logits = logits + dot(lower[half], jnp.concatenate([low, high], axis=0), NN)
            logits = logits + bias[...]
            grad_weights = dot(jnp.concatenate([values[half]] * 2, axis=1), stacked(grad, 2), NN)
            top = jnp.max(logits, axis=0, keepdims=True)
            exps = jnp.exp(logits - top)
            share = 1.0 / jnp.sum(exps, axis=0, keepdims=True)
            high, low = split(exps)
            mix = heads_dot(tt[mine], high, low, NN) * share
            mt[mine] = mix
            gt[mine] = heads_dot(grad * share, high, low, NT)
            delta = jnp.sum(grad * mix, axis=0, keepdims=True)
            high, low = split(exps * (grad_weights - delta))
            gq[mine] = heads_dot(kt[mine], high, low, NN) * share
            gk[mine] = heads_dot(query * share, high, low, NT)

    gv[...] = jnp.zeros(gv.shape, jnp.float32)
    for frame in range(frames):
        mine = rows_of(frame, SIZE)
        for chunk in range(patches // LANES):
            cols = rows_of(chunk, LANES)
            query, grad = qt[mine, cols], gt[mine, cols]
            weights, terms = [], []
            inner = jnp.zeros((1, LANES), jnp.float32)
            for key in visible_keys(frame):
                weight = wts[frame, frame - key : frame - key + 1, cols]
                term = jnp.sum(grad * vt[rows_of(key, SIZE), cols], axis=0, keepdims=True)
                inner = inner + weight * term
                weights.append(weight)
                terms.append(term)
            grad_query = gq[mine, cols]
            for key, weight, term in zip(visible_keys(frame), weights, terms):
                of = rows_of(key, SIZE)
                score = weight * (term - inner)
                grad_query = grad_query + score * kt[of, cols]
                gk[of, cols] = gk[of, cols] + score * query
                gv[of, cols] = gv[of, cols] + weight * grad
            gq[mine, cols] = grad_query * scale

    for group in range(groups):
        for number, ref in enumerate((mt, gq, gk, gv)):
            turned = ref[pair_rows(group)].T
            for part in range(parts):
                at = rows_of(number, rows)
                out_refs[back.index((group, part))][at] = turned[rows_of(part, rows)]


def exchange(blocks, order, patch_count):
    return [
        lax.ppermute(
            block,
            ("frame", "patch"),
            [
                (i * patch_count + j, (i ^ frame) * patch_count + (j ^ patch))
                for i in range(H // patch_count)
                for j in range(patch_count)
            ],
        )
        for block, (frame, patch) in zip(blocks, order)
    ]


def shards_by_head(queries, key_rows, value_rows, cotangent, lookback, window):
    frames_here, patches_here, model_width = queries.shape
    groups, parts = lax.axis_size("frame"), lax.axis_size("patch")
    frames, patches = frames_here * groups, patches_here * parts
    order = OUTWARD
    back = HOMEWARD
    vmem = pl.BlockSpec(memory_space=pltpu.VMEM)
    anywhere = pl.BlockSpec(memory_space=pl.ANY)
    dma = pltpu.SemaphoreType.DMA
    held = pltpu.VMEM(queries.shape, jnp.float32)
    smem = [pltpu.SMEM(window.shape, jnp.int32), pltpu.SMEM(lookback.shape, jnp.int32)]
    across = pltpu.VMEM((frames * SIZE, patches), jnp.float32)

    def blocks(count, rows):
        return [jax.ShapeDtypeStruct((rows, LANES), jnp.float32)] * count

    def params(mebibytes):
        return pltpu.CompilerParams(vmem_limit_bytes=mebibytes * 1024 * 1024)

    given = (window, lookback, queries, key_rows, value_rows, cotangent)
    packed = pl.pallas_call(
        lambda *refs: pack_kernel(order[1:], parts, *refs),
        out_shape=blocks(H - 1, 4 * patches_here + INFO),
        in_specs=[anywhere] * 6,
        out_specs=[vmem] * (H - 1),
        scratch_shapes=[held] * 4 + smem + [dma((10,))],
        compiler_params=params(56),
        name="pack_heads",
    )(*given)
    done = pl.pallas_call(
        lambda *refs: head_kernel(order, back, groups, parts, *refs),
        out_shape=blocks(H, 4 * patches_here),
        in_specs=[anywhere] * 6 + [vmem] * (H - 1),
        out_specs=[vmem] * H,
        scratch_shapes=[pltpu.VMEM((2, patches_here, LANES), jnp.float32)] * 4
        + [pltpu.VMEM((4 * patches_here, LANES), jnp.float32)]
        + smem
        + [pltpu.VMEM((groups, INFO, LANES), jnp.float32), dma((6,))]
        + [across] * 10
        + [
            pltpu.VMEM((frames, 8, patches), jnp.float32),
            pltpu.VMEM((patches, patches), jnp.float32),
        ],
        compiler_params=params(24),
        name="one_head",
    )(*given, *exchange(packed, order[1:], parts))
    return pl.pallas_call(
        lambda *refs: unpack_kernel(back, groups, parts, *refs),
        out_shape=[jax.ShapeDtypeStruct(queries.shape, jnp.float32)] * 4,
        in_specs=[vmem] * H,
        out_specs=[anywhere] * 4,
        scratch_shapes=[held] * 4 + [dma((4,))],
        compiler_params=params(40),
        name="unpack_heads",
    )(done[0], *exchange(done[1:], back[1:], parts))


def shards(queries, key_rows, value_rows, cotangent, lookback, window):
    frames_here, patches_here, model_width = queries.shape
    fits = (
        lax.axis_size("frame") * lax.axis_size("patch") == H
        and lax.axis_size("patch") == 4
        and frames_here == 2
        and patches_here == SIZE
        and model_width == H * SIZE
    )
    form = shards_by_head if fits else shards_general
    return tuple(form(queries, key_rows, value_rows, cotangent, lookback, window))


def solution(mesh):
    rows = P(("traj", "frame"), "patch", None)
    return jax.shard_map(
        shards,
        mesh=mesh,
        in_specs=(rows, rows, rows, rows, P(("traj", "frame")), P(("traj", "patch"), None)),
        out_specs=(rows,) * 4,
        check_vma=False,
    )
```

```python
import math

import jax
import jax.numpy as jnp
from jax import lax
from jax.experimental import pallas as pl
from jax.experimental.pallas import tpu as pltpu
from jax.sharding import PartitionSpec as P

H = 16
BLK = 16
LOOK = 6
REACH = 6


def shifted(x, axis, by):
    count = lax.axis_size(axis)
    pairs = [(i, i + by) for i in range(count) if 0 <= i + by < count]
    return lax.ppermute(x, axis, pairs)


def passed_along(block, axis, distance):
    devices = range(lax.axis_size(axis))
    route = [((i - distance) % len(devices), i) for i in devices]
    return lax.ppermute(block, axis, route)


def split_heads(tensor, size_head):
    return tensor.reshape(tensor.shape[0], tensor.shape[1], H, size_head)


def shards_general(queries, key_rows, value_rows, cotangent, lookback, window):
    frames_here, patches_here, model_width = queries.shape
    size_head = model_width // H
    score_scale = 1.0 / math.sqrt(size_head)
    highest = lax.Precision.HIGHEST
    frame_index = lax.axis_index("frame")
    cycle_depth = (LOOK + frames_here - 2) // frames_here
    earlier = []
    carried = (key_rows, value_rows)
    for distance in range(cycle_depth):
        carried = shifted((carried[0], carried[1]), "frame", 1)
        earlier.append(carried)
    bank_keys = jnp.concatenate(
        [earlier[cycle_depth - 1 - number][0] for number in range(cycle_depth)] + [key_rows], axis=0
    )
    bank_values = jnp.concatenate(
        [earlier[cycle_depth - 1 - number][1] for number in range(cycle_depth)] + [value_rows],
        axis=0,
    )
    bank_frames = bank_keys.shape[0]
    q_heads = split_heads(queries, size_head)
    key_heads = split_heads(bank_keys, size_head)
    value_heads = split_heads(bank_values, size_head)
    query_frame = frame_index * frames_here + jnp.arange(frames_here, dtype=jnp.int32)
    key_frame = (frame_index - cycle_depth) * frames_here + jnp.arange(bank_frames, dtype=jnp.int32)
    offset = query_frame[:, None] - key_frame[None, :]
    visible = (offset >= 0) & (offset < lookback[:, None]) & (key_frame[None, :] >= 0)
    scores = jnp.einsum("fphe,jphe->phfj", q_heads, key_heads, precision=highest) * score_scale
    scores = jnp.where(visible, scores, -jnp.inf)
    weights = jax.nn.softmax(scores, axis=-1)
    temporal = jnp.einsum("phfj,jphe->fphe", weights, value_heads, precision=highest).reshape(
        frames_here, patches_here, model_width
    )
    patch_count = lax.axis_size("patch")
    patch_index = lax.axis_index("patch")
    blocks_here = patches_here // BLK
    reach_devices = -(-REACH // blocks_here)
    offsets = []
    for stride in range(-reach_devices, reach_devices + 1):
        if all(((stride - earlier_step) % patch_count != 0 for earlier_step in offsets)):
            offsets.append(stride)
    entries = []
    running_base = 0
    for stride in offsets:
        count_here = blocks_here if stride != 0 and abs(stride) == reach_devices else blocks_here
        first_block = 0 if stride >= 0 else blocks_here - count_here
        entries.append((stride, first_block, count_here, running_base))
        running_base = running_base + count_here
    count_slots = running_base
    near_banks = []
    for stride, first_block, count_here, base_slot in entries:
        rows_from = first_block * BLK
        rows_to = (first_block + count_here) * BLK
        piece = (key_rows, temporal)
        if stride == 0:
            near_banks.append(piece)
        else:
            near_banks.append(passed_along((piece[0], piece[1]), "patch", -stride))
    near_keys = jnp.concatenate([entry[0] for entry in near_banks], axis=1)
    near_values = jnp.concatenate([entry[1] for entry in near_banks], axis=1)
    owner_device = window // blocks_here
    relative = (owner_device - patch_index) % patch_count
    base_of = jnp.zeros(window.shape, jnp.int32)
    first_of = jnp.zeros(window.shape, jnp.int32)
    for stride, first_block, count_here, base_slot in entries:
        matches = relative == stride % patch_count
        base_of = jnp.where(matches, base_slot, base_of)
        first_of = jnp.where(matches, first_block, first_of)
    slot_index = base_of + window % blocks_here - first_of
    window_count = window.shape[1]
    key_blocks = near_keys.reshape(frames_here, count_slots, BLK, model_width)
    value_blocks = near_values.reshape(frames_here, count_slots, BLK, model_width)

    def frame_step(frame_items):
        query_part, key_part, value_part, grad_part = frame_items
        key_win = key_part[slot_index].reshape(blocks_here, window_count * BLK, H, size_head)
        value_win = value_part[slot_index].reshape(blocks_here, window_count * BLK, H, size_head)
        query_win = query_part.reshape(blocks_here, BLK, H, size_head)
        grad_win = grad_part.reshape(blocks_here, BLK, H, size_head)
        logits = jnp.einsum("bxhe,byhe->bhxy", query_win, key_win, precision=highest) * score_scale
        attention = jax.nn.softmax(logits, axis=-1)
        mixed_rows = jnp.einsum("bhxy,byhe->bxhe", attention, value_win, precision=highest)
        grad_attention = jnp.einsum("bxhe,byhe->bhxy", grad_win, value_win, precision=highest)
        grad_logits = attention * (
            grad_attention - jnp.sum(attention * grad_attention, axis=-1, keepdims=True)
        )
        grad_query = (
            jnp.einsum("bhxy,byhe->bxhe", grad_logits, key_win, precision=highest) * score_scale
        )
        grad_key = (
            jnp.einsum("bhxy,bxhe->byhe", grad_logits, query_win, precision=highest) * score_scale
        )
        grad_value = jnp.einsum("bhxy,bxhe->byhe", attention, grad_win, precision=highest)
        block_shape = (blocks_here, window_count, BLK, model_width)
        key_back = (
            jnp.zeros((count_slots, BLK, model_width), jnp.float32)
            .at[slot_index]
            .add(grad_key.reshape(block_shape))
        )
        value_back = (
            jnp.zeros((count_slots, BLK, model_width), jnp.float32)
            .at[slot_index]
            .add(grad_value.reshape(block_shape))
        )
        return (
            mixed_rows.reshape(patches_here, model_width),
            grad_query.reshape(patches_here, model_width),
            key_back,
            value_back,
        )

    mixed, grad_query_space, key_back, value_back = lax.map(
        frame_step, (queries, key_blocks, value_blocks, cotangent)
    )
    key_back = key_back.reshape(frames_here, count_slots * BLK, model_width)
    value_back = value_back.reshape(frames_here, count_slots * BLK, model_width)
    grad_key_space = jnp.zeros(queries.shape, jnp.float32)
    grad_temporal = jnp.zeros(queries.shape, jnp.float32)
    for stride, first_block, count_here, base_slot in entries:
        slot_from = base_slot * BLK
        slot_to = (base_slot + count_here) * BLK
        returned = (key_back[:, slot_from:slot_to], value_back[:, slot_from:slot_to])
        if stride != 0:
            returned = passed_along((returned[0], returned[1]), "patch", stride)
        rows_from = first_block * BLK
        rows_to = (first_block + count_here) * BLK
        grad_key_space = grad_key_space.at[:, rows_from:rows_to].add(returned[0])
        grad_temporal = grad_temporal.at[:, rows_from:rows_to].add(returned[1])
    grad_heads = split_heads(grad_temporal, size_head)
    grad_weights = jnp.einsum("fphe,jphe->phfj", grad_heads, value_heads, precision=highest)
    grad_scores = weights * (grad_weights - jnp.sum(weights * grad_weights, axis=-1, keepdims=True))
    grad_query_time = (
        jnp.einsum("phfj,jphe->fphe", grad_scores, key_heads, precision=highest) * score_scale
    )
    key_terms = (
        jnp.einsum("phfj,fphe->jphe", grad_scores, q_heads, precision=highest) * score_scale
    ).reshape(cycle_depth + 1, frames_here, patches_here, model_width)
    value_terms = jnp.einsum("phfj,fphe->jphe", weights, grad_heads, precision=highest).reshape(
        cycle_depth + 1, frames_here, patches_here, model_width
    )
    carried = (key_terms[0], value_terms[0])
    for distance in range(1, cycle_depth + 1):
        carried = shifted((carried[0], carried[1]), "frame", -1)
        carried = (carried[0] + key_terms[distance], carried[1] + value_terms[distance])
    grad_key_time, grad_value_time = carried
    grad_queries = grad_query_space + grad_query_time.reshape(
        frames_here, patches_here, model_width
    )
    grad_keys = grad_key_space + grad_key_time
    return (mixed, grad_queries, grad_keys, grad_value_time)


LANES = 128
SIZE = LANES // 2
INFO = 8
OUTWARD = (
    (0, 0), (3, 3), (0, 1), (1, 0), (1, 2), (1, 1), (1, 3), (2, 2),
    (2, 1), (2, 3), (3, 0), (3, 2), (3, 1), (0, 2), (2, 0), (0, 3),
)
HOMEWARD = (
    (0, 0), (3, 3), (0, 1), (1, 0), (1, 2), (1, 1), (1, 3), (2, 2),
    (2, 1), (2, 3), (3, 0), (3, 2), (3, 1), (0, 2), (2, 0), (0, 3),
)
HIDDEN = -1e30
NN = ((1,), (0,))
NT = ((1,), (1,))


def interleave(first, second):
    axis = first.ndim - 1
    low = lax.broadcasted_iota(jnp.int32, first.shape, axis) < SIZE
    return (
        jnp.where(low, first, pltpu.roll(second, SIZE, axis)),
        jnp.where(low, pltpu.roll(first, SIZE, axis), second),
    )


def dot(a, b, dims):
    return lax.dot_general(a, b, (dims, ((), ())), preferred_element_type=jnp.float32)


def split(x):
    high = x.astype(jnp.bfloat16)
    return high, (x - high.astype(jnp.float32)).astype(jnp.bfloat16)


def stacked(x, times):
    high, low = split(x)
    return jnp.concatenate([high] * times + [low] * times, axis=0)


def heads_dot(x, high, low, dims):
    both = stacked(x, 1)
    out = dot(both, high, dims)
    return out[:SIZE] + (out[SIZE:] + dot(both[:SIZE], low, dims))


def place(partner, patch_count):
    frame = lax.bitwise_xor(lax.axis_index("frame"), partner[0])
    return frame * patch_count + lax.bitwise_xor(lax.axis_index("patch"), partner[1])


def columns_of(head):
    return pl.ds(pl.multiple_of(head // 2 * LANES, LANES), LANES)


def low_lanes(rows):
    return lax.broadcasted_iota(jnp.int32, (rows, LANES), 1) < SIZE


def side_by_side(ref, head, cols):
    odd = head % 2
    kept, moved = ref[odd, :, cols], ref[1 - odd, :, cols]
    low = low_lanes(kept.shape[0]).astype(jnp.int32)
    return jnp.where(low != odd, kept, pltpu.roll(moved, SIZE, 1))


def whole_numbers(window, lookback, rows):
    row = lax.broadcasted_iota(jnp.int32, (INFO, LANES), 0)
    lane = lax.broadcasted_iota(jnp.int32, (INFO, LANES), 1)
    info = jnp.zeros((INFO, LANES), jnp.int32)
    for block in range(rows // BLK):
        for column in range(window.shape[1]):
            at = block * BLK + (column // INFO) * SIZE
            here = (row == column % INFO) & (lane >= at) & (lane < at + BLK)
            info = jnp.where(here, window[block, column], info)
    for frame in range(2):
        here = (row == INFO - 2 + frame) & (lane >= SIZE)
        info = jnp.where(here, lookback[frame], info)
    return info.astype(jnp.float32)


def fetch(moves, sems):
    copies = [pltpu.make_async_copy(a, b, sems.at[n]) for n, (a, b) in enumerate(moves)]
    for copy in copies:
        copy.start()
    return copies


def pack_kernel(order, parts, window, lookback, *refs):
    arrays, out_refs = refs[:4], refs[4 : 3 + H]
    held, window_ref, lookback_ref, sems = refs[3 + H : 7 + H], *refs[7 + H :]
    moves = [(window, window_ref), (lookback, lookback_ref)]
    moves += [(a.at[frame], b.at[frame]) for a, b in zip(arrays, held) for frame in range(2)]
    copies = fetch(moves, sems)
    copies[0].wait()
    copies[1].wait()
    rows = held[0].shape[1]
    info = whole_numbers(window_ref, lookback_ref, rows)
    for ref in out_refs:
        ref[4 * rows :] = info
    for number, ref in enumerate(held):
        copies[2 + 2 * number].wait()
        copies[3 + 2 * number].wait()
        for partner, out_ref in zip(order, out_refs):
            head = place(partner, parts)
            out_ref[rows_of(number, rows)] = side_by_side(ref, head, columns_of(head))


def unpack_kernel(order, groups, parts, *refs):
    in_refs, out_refs, held, sems = refs[:H], refs[H : H + 4], refs[H + 4 : H + 8], refs[H + 8]
    rows = held[0].shape[1]
    copies = []
    for number, ref in enumerate(held):
        at = rows_of(number, rows)
        for frame in range(groups):
            for patch in range(0, parts, 2):
                head = place((frame, patch), parts)
                odd = jnp.full((rows, LANES), head % 2, jnp.int32) == 1
                here = in_refs[order.index((frame, patch))][at]
                there = in_refs[order.index((frame, patch + 1))][at]
                first, second = interleave(jnp.where(odd, there, here), jnp.where(odd, here, there))
                cols = columns_of(head)
                ref[0, :, cols] = first
                ref[1, :, cols] = second
        copies.append(pltpu.make_async_copy(ref, out_refs[number], sems.at[number]))
        copies[-1].start()
    for copy in copies:
        copy.wait()


def visible_keys(frame):
    return range(max(0, frame - LOOK + 1), frame + 1)


def rows_of(index, count):
    return slice(index * count, (index + 1) * count)


def head_kernel(order, back, groups, parts, window, lookback, *refs):
    arrays, in_refs, out_refs = refs[:4], refs[4 : 3 + H], refs[3 + H : 3 + 2 * H]
    held, own_ref, window_ref, lookback_ref, lookbacks, sems = refs[3 + 2 * H : 12 + 2 * H][:4], *refs[
        7 + 2 * H : 12 + 2 * H
    ]
    qt, kt, vt, ct, tt, mt, gt, gq, gk, gv, wts, bias, blocks = refs[12 + 2 * H :]
    rows = own_ref.shape[0] // 4
    frames, _, patches = wts.shape
    scale = 1.0 / math.sqrt(SIZE)

    head = place((0, 0), parts)
    moves = [(window, window_ref), (lookback, lookback_ref)]
    moves += [(a.at[:, :, columns_of(head)], b) for a, b in zip(arrays, held)]
    copies = fetch(moves, sems)

    def natural(number, group):
        at = rows_of(number, rows)
        found = [in_refs[order.index((group, part)) - 1][at] if group or part else own_ref[at] for part in range(parts)]
        return jnp.concatenate(found, axis=0)

    def tile(group, part):
        return in_refs[order.index((group, part)) - 1][4 * rows :] if group or part else info

    def pair_rows(group):
        at = lax.bitwise_xor(lax.axis_index("frame"), group) * LANES
        return pl.ds(pl.multiple_of(at, LANES), LANES)

    def turn(group):
        at = pair_rows(group)
        qt[at] = natural(0, group).T * scale
        kt[at] = natural(1, group).T
        vt[at] = natural(2, group).T
        ct[at] = natural(3, group).T
        lookbacks[lax.bitwise_xor(lax.axis_index("frame"), group)] = tile(group, 0)

    for group in range(1, groups):
        turn(group)
    for copy in copies:
        copy.wait()
    for number, ref in enumerate(held):
        own_ref[rows_of(number, rows)] = side_by_side(ref, head, slice(None))
    info = whole_numbers(window_ref, lookback_ref, rows)
    turn(0)

    sides = [interleave(tile(0, part), tile(0, part + 1)) for part in range(0, parts, 2)]
    first = jnp.concatenate([side[0] for side in sides], axis=1)
    last = jnp.concatenate([side[1] for side in sides], axis=1)
    count = rows // BLK
    block = lax.broadcasted_iota(jnp.int32, (parts * count, patches), 0)
    block = lax.bitwise_xor(block // count, lax.axis_index("patch")) * count + block % count
    block = block.astype(jnp.float32)
    seen = block == first[0:1]
    for column in range(1, window.shape[1]):
        of = first if column < INFO else last
        seen = seen | (block == of[column % INFO : column % INFO + 1])
    mask = jnp.where(seen, 0.0, HIDDEN).astype(jnp.bfloat16)
    spare = jnp.zeros((LANES - parts * count, patches), jnp.bfloat16)
    bias[...] = jnp.concatenate([mask, spare], axis=0)
    key_block = lax.broadcasted_iota(jnp.int32, (patches, LANES), 0) // BLK
    lane = lax.broadcasted_iota(jnp.int32, (patches, LANES), 1)
    blocks[...] = jnp.where(key_block == lane, 1.0, 0.0).astype(jnp.bfloat16)

    def look_back(frame):
        _, given = interleave(lookbacks[frame // 2], lookbacks[frame // 2])
        at = INFO - 2 + frame % 2
        seen_frames = given[at : at + 1]
        for chunk in range(patches // LANES):
            cols = rows_of(chunk, LANES)
            query = qt[rows_of(frame, SIZE), cols]
            keys = visible_keys(frame)
            scores = []
            for key in keys:
                score = jnp.sum(query * kt[rows_of(key, SIZE), cols], axis=0, keepdims=True)
                scores.append(jnp.where(seen_frames > float(frame - key), score, -jnp.inf))
            top = scores[0]
            for score in scores[1:]:
                top = jnp.maximum(top, score)
            exps = [jnp.exp(score - top) for score in scores]
            total = exps[0]
            for term in exps[1:]:
                total = total + term
            value = jnp.zeros((SIZE, LANES), jnp.float32)
            for key, term in zip(keys, exps):
                weight = term / total
                wts[frame, frame - key : frame - key + 1, cols] = weight
                value = value + weight * vt[rows_of(key, SIZE), cols]
            tt[rows_of(frame, SIZE), cols] = value

    state = {}

    def products(frame):
        mine = rows_of(frame, SIZE)
        if frame % 2 == 0:
            at = rows_of(frame // 2, LANES)
            keys = kt[at].T
            high = keys.astype(jnp.bfloat16).astype(jnp.float32)
            low = keys - high
            mid = low.astype(jnp.bfloat16).astype(jnp.float32)
            upper = [x.astype(jnp.bfloat16) for x in interleave(high, mid)]
            lower = [x.astype(jnp.bfloat16) for x in interleave(high, low - mid)]
            value = tt[at].T
            high = value.astype(jnp.bfloat16).astype(jnp.float32)
            values = [x.astype(jnp.bfloat16) for x in interleave(high, value - high)]
            state["pair"] = list(zip(upper, lower, values))
        upper, lower, value = state["pair"][frame % 2]
        query = qt[mine]
        high, mid = split(query)
        low = query - high.astype(jnp.float32) - mid.astype(jnp.float32)
        low = low.astype(jnp.bfloat16)
        logits = dot(
            jnp.concatenate([upper] * 2, axis=1),
            jnp.concatenate([high, high, mid, mid], axis=0),
            NN,
        )
        logits = logits + dot(
            jnp.concatenate([lower, blocks[...]], axis=1),
            jnp.concatenate([low, high, bias[...]], axis=0),
            NN,
        )
        grad_weights = dot(jnp.concatenate([value] * 2, axis=1), stacked(ct[mine], 2), NN)
        state[frame] = logits, grad_weights

    def weigh(frame):
        logits, grad_weights = state[frame]
        top = jnp.max(logits, axis=0, keepdims=True)
        exps = jnp.exp(logits - top)
        share = 1.0 / jnp.sum(exps, axis=0, keepdims=True)
        state[frame] = exps, *split(exps), share, grad_weights

    def mix(frame):
        mine = rows_of(frame, SIZE)
        exps, high, low, share, grad_weights = state[frame]
        mt[mine] = heads_dot(tt[mine], high, low, NN) * share
        gt[mine] = heads_dot(ct[mine] * share, high, low, NT)

    def differ(frame):
        mine = rows_of(frame, SIZE)
        exps, _, _, share, grad_weights = state[frame]
        delta = jnp.sum(ct[mine] * mt[mine], axis=0, keepdims=True)
        state[frame] = *split(exps * (grad_weights - delta)), share

    def finish(frame):
        mine = rows_of(frame, SIZE)
        high, low, share = state.pop(frame)
        gq[mine] = heads_dot(kt[mine], high, low, NN) * share
        gk[mine] = heads_dot(qt[mine] * share, high, low, NT)

    def hand_back(frame):
        mine = rows_of(frame, SIZE)
        for chunk in range(patches // LANES):
            cols = rows_of(chunk, LANES)
            query, grad = qt[mine, cols], gt[mine, cols]
            weights, terms = [], []
            inner = jnp.zeros((1, LANES), jnp.float32)
            for key in visible_keys(frame):
                weight = wts[frame, frame - key : frame - key + 1, cols]
                term = jnp.sum(grad * vt[rows_of(key, SIZE), cols], axis=0, keepdims=True)
                inner = inner + weight * term
                weights.append(weight)
                terms.append(term)
            grad_query = gq[mine, cols]
            for key, weight, term in zip(visible_keys(frame), weights, terms):
                of = rows_of(key, SIZE)
                score = weight * (term - inner)
                grad_query = grad_query + score * kt[of, cols]
                gk[of, cols] = gk[of, cols] + score * query
                if key == frame:
                    gv[of, cols] = weight * grad
                else:
                    gv[of, cols] = gv[of, cols] + weight * grad
            gq[mine, cols] = grad_query * scale

    for step in range(frames + 5):
        for late, does in (
            (0, look_back),
            (2, products),
            (3, weigh),
            (4, differ),
            (3, mix),
            (4, finish),
            (5, hand_back),
        ):
            if 0 <= step - late < frames:
                does(step - late)

    for group in range(groups):
        for number, ref in enumerate((mt, gq, gk, gv)):
            turned = ref[pair_rows(group)].T
            for part in range(parts):
                at = rows_of(number, rows)
                out_refs[back.index((group, part))][at] = turned[rows_of(part, rows)]


def exchange(blocks, order, patch_count):
    return [
        lax.ppermute(
            block,
            ("frame", "patch"),
            [
                (i * patch_count + j, (i ^ frame) * patch_count + (j ^ patch))
                for i in range(H // patch_count)
                for j in range(patch_count)
            ],
        )
        for block, (frame, patch) in zip(blocks, order)
    ]


def shards_by_head(queries, key_rows, value_rows, cotangent, lookback, window):
    frames_here, patches_here, model_width = queries.shape
    groups, parts = lax.axis_size("frame"), lax.axis_size("patch")
    frames, patches = frames_here * groups, patches_here * parts
    order = OUTWARD
    back = HOMEWARD
    vmem = pl.BlockSpec(memory_space=pltpu.VMEM)
    anywhere = pl.BlockSpec(memory_space=pl.ANY)
    dma = pltpu.SemaphoreType.DMA
    held = pltpu.VMEM(queries.shape, jnp.float32)
    smem = [pltpu.SMEM(window.shape, jnp.int32), pltpu.SMEM(lookback.shape, jnp.int32)]
    across = pltpu.VMEM((frames * SIZE, patches), jnp.float32)

    def blocks(count, rows):
        return [jax.ShapeDtypeStruct((rows, LANES), jnp.float32)] * count

    def params(mebibytes):
        return pltpu.CompilerParams(vmem_limit_bytes=mebibytes * 1024 * 1024)

    given = (window, lookback, queries, key_rows, value_rows, cotangent)
    packed = pl.pallas_call(
        lambda *refs: pack_kernel(order[1:], parts, *refs),
        out_shape=blocks(H - 1, 4 * patches_here + INFO),
        in_specs=[anywhere] * 6,
        out_specs=[vmem] * (H - 1),
        scratch_shapes=[held] * 4 + smem + [dma((10,))],
        compiler_params=params(56),
        name="pack_heads",
    )(*given)
    done = pl.pallas_call(
        lambda *refs: head_kernel(order, back, groups, parts, *refs),
        out_shape=blocks(H, 4 * patches_here),
        in_specs=[anywhere] * 6 + [vmem] * (H - 1),
        out_specs=[vmem] * H,
        scratch_shapes=[pltpu.VMEM((2, patches_here, LANES), jnp.float32)] * 4
        + [pltpu.VMEM((4 * patches_here, LANES), jnp.float32)]
        + smem
        + [pltpu.VMEM((groups, INFO, LANES), jnp.float32), dma((6,))]
        + [across] * 10
        + [
            pltpu.VMEM((frames, 8, patches), jnp.float32),
            pltpu.VMEM((LANES, patches), jnp.bfloat16),
            pltpu.VMEM((patches, LANES), jnp.bfloat16),
        ],
        compiler_params=params(24),
        name="one_head",
    )(*given, *exchange(packed, order[1:], parts))
    return pl.pallas_call(
        lambda *refs: unpack_kernel(back, groups, parts, *refs),
        out_shape=[jax.ShapeDtypeStruct(queries.shape, jnp.float32)] * 4,
        in_specs=[vmem] * H,
        out_specs=[anywhere] * 4,
        scratch_shapes=[held] * 4 + [dma((4,))],
        compiler_params=params(40),
        name="unpack_heads",
    )(done[0], *exchange(done[1:], back[1:], parts))


def shards(queries, key_rows, value_rows, cotangent, lookback, window):
    frames_here, patches_here, model_width = queries.shape
    fits = (
        lax.axis_size("frame") * lax.axis_size("patch") == H
        and lax.axis_size("patch") == 4
        and frames_here == 2
        and patches_here == SIZE
        and model_width == H * SIZE
    )
    form = shards_by_head if fits else shards_general
    return tuple(form(queries, key_rows, value_rows, cotangent, lookback, window))


def solution(mesh):
    rows = P(("traj", "frame"), "patch", None)
    return jax.shard_map(
        shards,
        mesh=mesh,
        in_specs=(rows, rows, rows, rows, P(("traj", "frame")), P(("traj", "patch"), None)),
        out_specs=(rows,) * 4,
        check_vma=False,
    )
```

```python
import math

import jax
import jax.numpy as jnp
from jax import lax
from jax.experimental import pallas as pl
from jax.experimental.pallas import tpu as pltpu
from jax.sharding import PartitionSpec as P

H = 16
BLK = 16
LOOK = 6
REACH = 6


def shifted(x, axis, by):
    count = lax.axis_size(axis)
    pairs = [(i, i + by) for i in range(count) if 0 <= i + by < count]
    return lax.ppermute(x, axis, pairs)


def passed_along(block, axis, distance):
    devices = range(lax.axis_size(axis))
    route = [((i - distance) % len(devices), i) for i in devices]
    return lax.ppermute(block, axis, route)


def split_heads(tensor, size_head):
    return tensor.reshape(tensor.shape[0], tensor.shape[1], H, size_head)


def shards_general(queries, key_rows, value_rows, cotangent, lookback, window):
    frames_here, patches_here, model_width = queries.shape
    size_head = model_width // H
    score_scale = 1.0 / math.sqrt(size_head)
    highest = lax.Precision.HIGHEST
    frame_index = lax.axis_index("frame")
    cycle_depth = (LOOK + frames_here - 2) // frames_here
    earlier = []
    carried = (key_rows, value_rows)
    for distance in range(cycle_depth):
        carried = shifted((carried[0], carried[1]), "frame", 1)
        earlier.append(carried)
    bank_keys = jnp.concatenate(
        [earlier[cycle_depth - 1 - number][0] for number in range(cycle_depth)] + [key_rows], axis=0
    )
    bank_values = jnp.concatenate(
        [earlier[cycle_depth - 1 - number][1] for number in range(cycle_depth)] + [value_rows],
        axis=0,
    )
    bank_frames = bank_keys.shape[0]
    q_heads = split_heads(queries, size_head)
    key_heads = split_heads(bank_keys, size_head)
    value_heads = split_heads(bank_values, size_head)
    query_frame = frame_index * frames_here + jnp.arange(frames_here, dtype=jnp.int32)
    key_frame = (frame_index - cycle_depth) * frames_here + jnp.arange(bank_frames, dtype=jnp.int32)
    offset = query_frame[:, None] - key_frame[None, :]
    visible = (offset >= 0) & (offset < lookback[:, None]) & (key_frame[None, :] >= 0)
    scores = jnp.einsum("fphe,jphe->phfj", q_heads, key_heads, precision=highest) * score_scale
    scores = jnp.where(visible, scores, -jnp.inf)
    weights = jax.nn.softmax(scores, axis=-1)
    temporal = jnp.einsum("phfj,jphe->fphe", weights, value_heads, precision=highest).reshape(
        frames_here, patches_here, model_width
    )
    patch_count = lax.axis_size("patch")
    patch_index = lax.axis_index("patch")
    blocks_here = patches_here // BLK
    reach_devices = -(-REACH // blocks_here)
    offsets = []
    for stride in range(-reach_devices, reach_devices + 1):
        if all(((stride - earlier_step) % patch_count != 0 for earlier_step in offsets)):
            offsets.append(stride)
    entries = []
    running_base = 0
    for stride in offsets:
        count_here = blocks_here if stride != 0 and abs(stride) == reach_devices else blocks_here
        first_block = 0 if stride >= 0 else blocks_here - count_here
        entries.append((stride, first_block, count_here, running_base))
        running_base = running_base + count_here
    count_slots = running_base
    near_banks = []
    for stride, first_block, count_here, base_slot in entries:
        rows_from = first_block * BLK
        rows_to = (first_block + count_here) * BLK
        piece = (key_rows, temporal)
        if stride == 0:
            near_banks.append(piece)
        else:
            near_banks.append(passed_along((piece[0], piece[1]), "patch", -stride))
    near_keys = jnp.concatenate([entry[0] for entry in near_banks], axis=1)
    near_values = jnp.concatenate([entry[1] for entry in near_banks], axis=1)
    owner_device = window // blocks_here
    relative = (owner_device - patch_index) % patch_count
    base_of = jnp.zeros(window.shape, jnp.int32)
    first_of = jnp.zeros(window.shape, jnp.int32)
    for stride, first_block, count_here, base_slot in entries:
        matches = relative == stride % patch_count
        base_of = jnp.where(matches, base_slot, base_of)
        first_of = jnp.where(matches, first_block, first_of)
    slot_index = base_of + window % blocks_here - first_of
    window_count = window.shape[1]
    key_blocks = near_keys.reshape(frames_here, count_slots, BLK, model_width)
    value_blocks = near_values.reshape(frames_here, count_slots, BLK, model_width)

    def frame_step(frame_items):
        query_part, key_part, value_part, grad_part = frame_items
        key_win = key_part[slot_index].reshape(blocks_here, window_count * BLK, H, size_head)
        value_win = value_part[slot_index].reshape(blocks_here, window_count * BLK, H, size_head)
        query_win = query_part.reshape(blocks_here, BLK, H, size_head)
        grad_win = grad_part.reshape(blocks_here, BLK, H, size_head)
        logits = jnp.einsum("bxhe,byhe->bhxy", query_win, key_win, precision=highest) * score_scale
        attention = jax.nn.softmax(logits, axis=-1)
        mixed_rows = jnp.einsum("bhxy,byhe->bxhe", attention, value_win, precision=highest)
        grad_attention = jnp.einsum("bxhe,byhe->bhxy", grad_win, value_win, precision=highest)
        grad_logits = attention * (
            grad_attention - jnp.sum(attention * grad_attention, axis=-1, keepdims=True)
        )
        grad_query = (
            jnp.einsum("bhxy,byhe->bxhe", grad_logits, key_win, precision=highest) * score_scale
        )
        grad_key = (
            jnp.einsum("bhxy,bxhe->byhe", grad_logits, query_win, precision=highest) * score_scale
        )
        grad_value = jnp.einsum("bhxy,bxhe->byhe", attention, grad_win, precision=highest)
        block_shape = (blocks_here, window_count, BLK, model_width)
        key_back = (
            jnp.zeros((count_slots, BLK, model_width), jnp.float32)
            .at[slot_index]
            .add(grad_key.reshape(block_shape))
        )
        value_back = (
            jnp.zeros((count_slots, BLK, model_width), jnp.float32)
            .at[slot_index]
            .add(grad_value.reshape(block_shape))
        )
        return (
            mixed_rows.reshape(patches_here, model_width),
            grad_query.reshape(patches_here, model_width),
            key_back,
            value_back,
        )

    mixed, grad_query_space, key_back, value_back = lax.map(
        frame_step, (queries, key_blocks, value_blocks, cotangent)
    )
    key_back = key_back.reshape(frames_here, count_slots * BLK, model_width)
    value_back = value_back.reshape(frames_here, count_slots * BLK, model_width)
    grad_key_space = jnp.zeros(queries.shape, jnp.float32)
    grad_temporal = jnp.zeros(queries.shape, jnp.float32)
    for stride, first_block, count_here, base_slot in entries:
        slot_from = base_slot * BLK
        slot_to = (base_slot + count_here) * BLK
        returned = (key_back[:, slot_from:slot_to], value_back[:, slot_from:slot_to])
        if stride != 0:
            returned = passed_along((returned[0], returned[1]), "patch", stride)
        rows_from = first_block * BLK
        rows_to = (first_block + count_here) * BLK
        grad_key_space = grad_key_space.at[:, rows_from:rows_to].add(returned[0])
        grad_temporal = grad_temporal.at[:, rows_from:rows_to].add(returned[1])
    grad_heads = split_heads(grad_temporal, size_head)
    grad_weights = jnp.einsum("fphe,jphe->phfj", grad_heads, value_heads, precision=highest)
    grad_scores = weights * (grad_weights - jnp.sum(weights * grad_weights, axis=-1, keepdims=True))
    grad_query_time = (
        jnp.einsum("phfj,jphe->fphe", grad_scores, key_heads, precision=highest) * score_scale
    )
    key_terms = (
        jnp.einsum("phfj,fphe->jphe", grad_scores, q_heads, precision=highest) * score_scale
    ).reshape(cycle_depth + 1, frames_here, patches_here, model_width)
    value_terms = jnp.einsum("phfj,fphe->jphe", weights, grad_heads, precision=highest).reshape(
        cycle_depth + 1, frames_here, patches_here, model_width
    )
    carried = (key_terms[0], value_terms[0])
    for distance in range(1, cycle_depth + 1):
        carried = shifted((carried[0], carried[1]), "frame", -1)
        carried = (carried[0] + key_terms[distance], carried[1] + value_terms[distance])
    grad_key_time, grad_value_time = carried
    grad_queries = grad_query_space + grad_query_time.reshape(
        frames_here, patches_here, model_width
    )
    grad_keys = grad_key_space + grad_key_time
    return (mixed, grad_queries, grad_keys, grad_value_time)


LANES = 128
SIZE = LANES // 2
INFO = 8
OUTWARD = (
    (0, 0), (2, 3), (1, 1), (1, 0), (0, 2), (0, 1), (0, 3), (3, 2),
    (3, 1), (1, 2), (2, 1), (2, 0), (2, 2), (3, 3), (3, 0), (1, 3),
)
HOMEWARD = (
    (0, 0), (2, 3), (1, 1), (1, 0), (0, 2), (0, 1), (0, 3), (3, 2),
    (3, 1), (3, 3), (2, 0), (2, 2), (2, 1), (1, 2), (3, 0), (1, 3),
)
FIRST = 5
HIDDEN = -1e30
NN = ((1,), (0,))
NT = ((1,), (1,))


def interleave(first, second):
    axis = first.ndim - 1
    low = lax.broadcasted_iota(jnp.int32, first.shape, axis) < SIZE
    return (
        jnp.where(low, first, pltpu.roll(second, SIZE, axis)),
        jnp.where(low, pltpu.roll(first, SIZE, axis), second),
    )


def dot(a, b, dims):
    return lax.dot_general(a, b, (dims, ((), ())), preferred_element_type=jnp.float32)


def split(x):
    high = x.astype(jnp.bfloat16)
    return high, (x - high.astype(jnp.float32)).astype(jnp.bfloat16)


def stacked(x, times):
    high, low = split(x)
    return jnp.concatenate([high] * times + [low] * times, axis=0)


def heads_dot(x, high, low, dims):
    both = stacked(x, 1)
    out = dot(both, high, dims)
    return out[:SIZE] + (out[SIZE:] + dot(both[:SIZE], low, dims))


def place(partner, patch_count):
    frame = lax.bitwise_xor(lax.axis_index("frame"), partner[0])
    return frame * patch_count + lax.bitwise_xor(lax.axis_index("patch"), partner[1])


def columns_of(head):
    return pl.ds(pl.multiple_of(head // 2 * LANES, LANES), LANES)


def low_lanes(rows):
    return lax.broadcasted_iota(jnp.int32, (rows, LANES), 1) < SIZE


def side_by_side(ref, head, cols):
    odd = head % 2
    kept, moved = ref[odd, :, cols], ref[1 - odd, :, cols]
    low = low_lanes(kept.shape[0]).astype(jnp.int32)
    return jnp.where(low != odd, kept, pltpu.roll(moved, SIZE, 1))


def whole_numbers(window, lookback, rows):
    row = lax.broadcasted_iota(jnp.int32, (INFO, LANES), 0)
    lane = lax.broadcasted_iota(jnp.int32, (INFO, LANES), 1)
    info = jnp.zeros((INFO, LANES), jnp.int32)
    for block in range(rows // BLK):
        for column in range(window.shape[1]):
            at = block * BLK + (column // INFO) * SIZE
            here = (row == column % INFO) & (lane >= at) & (lane < at + BLK)
            info = jnp.where(here, window[block, column], info)
    for frame in range(2):
        here = (row == INFO - 2 + frame) & (lane >= SIZE)
        info = jnp.where(here, lookback[frame], info)
    return info.astype(jnp.float32)


def fetch(moves, sems):
    copies = [pltpu.make_async_copy(a, b, sems.at[n]) for n, (a, b) in enumerate(moves)]
    for copy in copies:
        copy.start()
    return copies


def pack_kernel(order, parts, window, lookback, *refs):
    arrays, out_refs, refs = refs[:4], refs[4 : 4 + len(order)], refs[4 + len(order) :]
    held, window_ref, lookback_ref, sems = refs[:4], *refs[4:]
    moves = [(window, window_ref), (lookback, lookback_ref)]
    moves += [(a.at[frame], b.at[frame]) for a, b in zip(arrays, held) for frame in range(2)]
    copies = fetch(moves, sems)
    copies[0].wait()
    copies[1].wait()
    rows = held[0].shape[1]
    info = whole_numbers(window_ref, lookback_ref, rows)
    for ref in out_refs:
        ref[4 * rows :] = info
    for number, ref in enumerate(held):
        copies[2 + 2 * number].wait()
        copies[3 + 2 * number].wait()
        for partner, out_ref in zip(order, out_refs):
            head = place(partner, parts)
            out_ref[rows_of(number, rows)] = side_by_side(ref, head, columns_of(head))


def unpack_kernel(order, groups, parts, *refs):
    in_refs, out_refs, held, sems = refs[:H], refs[H : H + 4], refs[H + 4], refs[H + 5]
    rows = held.shape[3]
    pairs = [(frame, patch) for frame in range(groups) for patch in range(0, parts, 2)]
    copies = []
    for n, (frame, patch) in enumerate(pairs):
        head = place((frame, patch), parts)
        odd = jnp.full((rows, LANES), head % 2, jnp.int32) == 1
        for m, out_ref in enumerate(out_refs):
            at = rows_of(m, rows)
            here = in_refs[order.index((frame, patch))][at]
            there = in_refs[order.index((frame, patch + 1))][at]
            held[n, m, 0], held[n, m, 1] = interleave(
                jnp.where(odd, there, here), jnp.where(odd, here, there)
            )
            copies.append(
                pltpu.make_async_copy(
                    held.at[n, m], out_ref.at[:, :, columns_of(head)], sems.at[4 * n + m]
                )
            )
            copies[-1].start()
    for copy in copies:
        copy.wait()


def visible_keys(frame):
    return range(max(0, frame - LOOK + 1), frame + 1)


def rows_of(index, count):
    return slice(index * count, (index + 1) * count)


def head_kernel(order, back, groups, parts, window, lookback, *refs):
    arrays, in_refs, out_refs = refs[:4], refs[4 : 3 + H], refs[3 + H : 3 + 2 * H]
    held, own_ref, window_ref, lookback_ref, lookbacks, sems = refs[3 + 2 * H : 12 + 2 * H][:4], *refs[
        7 + 2 * H : 12 + 2 * H
    ]
    qt, kt, vt, ct, tt, mt, gt, gq, gk, gv, wts, bias, blocks = refs[12 + 2 * H :]
    rows = own_ref.shape[0] // 4
    frames, _, patches = wts.shape
    scale = 1.0 / math.sqrt(SIZE)

    head = place((0, 0), parts)
    moves = [(window, window_ref), (lookback, lookback_ref)]
    moves += [(a.at[:, :, columns_of(head)], b) for a, b in zip(arrays, held)]
    copies = fetch(moves, sems)

    def natural(number, group):
        at = rows_of(number, rows)
        found = [in_refs[order.index((group, part)) - 1][at] if group or part else own_ref[at] for part in range(parts)]
        return jnp.concatenate(found, axis=0)

    def tile(group, part):
        return in_refs[order.index((group, part)) - 1][4 * rows :] if group or part else info

    def pair_rows(group):
        at = lax.bitwise_xor(lax.axis_index("frame"), group) * LANES
        return pl.ds(pl.multiple_of(at, LANES), LANES)

    def turn(group):
        at = pair_rows(group)
        qt[at] = natural(0, group).T * scale
        kt[at] = natural(1, group).T
        vt[at] = natural(2, group).T
        ct[at] = natural(3, group).T
        lookbacks[lax.bitwise_xor(lax.axis_index("frame"), group)] = tile(group, 0)

    for group in range(1, groups):
        turn(group)
    for copy in copies:
        copy.wait()
    for number, ref in enumerate(held):
        own_ref[rows_of(number, rows)] = side_by_side(ref, head, slice(None))
    info = whole_numbers(window_ref, lookback_ref, rows)
    turn(0)

    sides = [interleave(tile(0, part), tile(0, part + 1)) for part in range(0, parts, 2)]
    first = jnp.concatenate([side[0] for side in sides], axis=1)
    last = jnp.concatenate([side[1] for side in sides], axis=1)
    count = rows // BLK
    block = lax.broadcasted_iota(jnp.int32, (parts * count, patches), 0)
    block = lax.bitwise_xor(block // count, lax.axis_index("patch")) * count + block % count
    block = block.astype(jnp.float32)
    seen = block == first[0:1]
    for column in range(1, window.shape[1]):
        of = first if column < INFO else last
        seen = seen | (block == of[column % INFO : column % INFO + 1])
    mask = jnp.where(seen, 0.0, HIDDEN).astype(jnp.bfloat16)
    spare = jnp.zeros((LANES - parts * count, patches), jnp.bfloat16)
    bias[...] = jnp.concatenate([mask, spare], axis=0)
    key_block = lax.broadcasted_iota(jnp.int32, (patches, LANES), 0) // BLK
    lane = lax.broadcasted_iota(jnp.int32, (patches, LANES), 1)
    blocks[...] = jnp.where(key_block == lane, 1.0, 0.0).astype(jnp.bfloat16)

    def look_back(frame):
        _, given = interleave(lookbacks[frame // 2], lookbacks[frame // 2])
        at = INFO - 2 + frame % 2
        seen_frames = given[at : at + 1]
        for chunk in range(patches // LANES):
            cols = rows_of(chunk, LANES)
            query = qt[rows_of(frame, SIZE), cols]
            keys = visible_keys(frame)
            scores = []
            for key in keys:
                score = jnp.sum(query * kt[rows_of(key, SIZE), cols], axis=0, keepdims=True)
                scores.append(jnp.where(seen_frames > float(frame - key), score, -jnp.inf))
            top = scores[0]
            for score in scores[1:]:
                top = jnp.maximum(top, score)
            exps = [jnp.exp(score - top) for score in scores]
            total = exps[0]
            for term in exps[1:]:
                total = total + term
            value = jnp.zeros((SIZE, LANES), jnp.float32)
            for key, term in zip(keys, exps):
                weight = term / total
                wts[frame, frame - key : frame - key + 1, cols] = weight
                value = value + weight * vt[rows_of(key, SIZE), cols]
            tt[rows_of(frame, SIZE), cols] = value

    state = {}

    def products(frame):
        mine = rows_of(frame, SIZE)
        if frame % 2 == 0:
            at = rows_of(frame // 2, LANES)
            keys = kt[at].T
            high = keys.astype(jnp.bfloat16).astype(jnp.float32)
            low = keys - high
            mid = low.astype(jnp.bfloat16).astype(jnp.float32)
            upper = [x.astype(jnp.bfloat16) for x in interleave(high, mid)]
            lower = [x.astype(jnp.bfloat16) for x in interleave(high, low - mid)]
            value = tt[at].T
            high = value.astype(jnp.bfloat16).astype(jnp.float32)
            values = [x.astype(jnp.bfloat16) for x in interleave(high, value - high)]
            state["pair"] = list(zip(upper, lower, values))
        upper, lower, value = state["pair"][frame % 2]
        query = qt[mine]
        high, mid = split(query)
        low = query - high.astype(jnp.float32) - mid.astype(jnp.float32)
        low = low.astype(jnp.bfloat16)
        logits = dot(
            jnp.concatenate([upper] * 2, axis=1),
            jnp.concatenate([high, high, mid, mid], axis=0),
            NN,
        )
        logits = logits + dot(
            jnp.concatenate([lower, blocks[...]], axis=1),
            jnp.concatenate([low, high, bias[...]], axis=0),
            NN,
        )
        grad_weights = dot(jnp.concatenate([value] * 2, axis=1), stacked(ct[mine], 2), NN)
        state[frame] = logits, grad_weights

    def weigh(frame):
        logits, grad_weights = state[frame]
        top = jnp.max(logits, axis=0, keepdims=True)
        exps = jnp.exp(logits - top)
        share = 1.0 / jnp.sum(exps, axis=0, keepdims=True)
        state[frame] = exps, *split(exps), share, grad_weights

    def mix(frame):
        mine = rows_of(frame, SIZE)
        exps, high, low, share, grad_weights = state[frame]
        mt[mine] = heads_dot(tt[mine], high, low, NN) * share
        gt[mine] = heads_dot(ct[mine] * share, high, low, NT)

    def differ(frame):
        mine = rows_of(frame, SIZE)
        exps, _, _, share, grad_weights = state[frame]
        delta = jnp.sum(ct[mine] * mt[mine], axis=0, keepdims=True)
        state[frame] = *split(exps * (grad_weights - delta)), share

    def finish(frame):
        mine = rows_of(frame, SIZE)
        high, low, share = state.pop(frame)
        gq[mine] = heads_dot(kt[mine], high, low, NN) * share
        gk[mine] = heads_dot(qt[mine] * share, high, low, NT)

    def hand_back(frame):
        mine = rows_of(frame, SIZE)
        for chunk in range(patches // LANES):
            cols = rows_of(chunk, LANES)
            query, grad = qt[mine, cols], gt[mine, cols]
            weights, terms = [], []
            inner = jnp.zeros((1, LANES), jnp.float32)
            for key in visible_keys(frame):
                weight = wts[frame, frame - key : frame - key + 1, cols]
                term = jnp.sum(grad * vt[rows_of(key, SIZE), cols], axis=0, keepdims=True)
                inner = inner + weight * term
                weights.append(weight)
                terms.append(term)
            grad_query = gq[mine, cols]
            for key, weight, term in zip(visible_keys(frame), weights, terms):
                of = rows_of(key, SIZE)
                score = weight * (term - inner)
                grad_query = grad_query + score * kt[of, cols]
                gk[of, cols] = gk[of, cols] + score * query
                if key == frame:
                    gv[of, cols] = weight * grad
                else:
                    gv[of, cols] = gv[of, cols] + weight * grad
            gq[mine, cols] = grad_query * scale

    for step in range(frames + 5):
        for late, does in (
            (0, look_back),
            (2, products),
            (3, weigh),
            (4, differ),
            (3, mix),
            (4, finish),
            (5, hand_back),
        ):
            if 0 <= step - late < frames:
                does(step - late)

    for group in range(groups):
        for number, ref in enumerate((mt, gq, gk, gv)):
            turned = ref[pair_rows(group)].T
            for part in range(parts):
                at = rows_of(number, rows)
                out_refs[back.index((group, part))][at] = turned[rows_of(part, rows)]


def exchange(blocks, order, patch_count):
    return [
        lax.ppermute(
            block,
            ("frame", "patch"),
            [
                (i * patch_count + j, (i ^ frame) * patch_count + (j ^ patch))
                for i in range(H // patch_count)
                for j in range(patch_count)
            ],
        )
        for block, (frame, patch) in zip(blocks, order)
    ]


def shards_by_head(queries, key_rows, value_rows, cotangent, lookback, window):
    frames_here, patches_here, model_width = queries.shape
    groups, parts = lax.axis_size("frame"), lax.axis_size("patch")
    frames, patches = frames_here * groups, patches_here * parts
    order = OUTWARD
    back = HOMEWARD
    vmem = pl.BlockSpec(memory_space=pltpu.VMEM)
    anywhere = pl.BlockSpec(memory_space=pl.ANY)
    dma = pltpu.SemaphoreType.DMA
    held = pltpu.VMEM(queries.shape, jnp.float32)
    smem = [pltpu.SMEM(window.shape, jnp.int32), pltpu.SMEM(lookback.shape, jnp.int32)]
    across = pltpu.VMEM((frames * SIZE, patches), jnp.float32)

    def blocks(count, rows):
        return [jax.ShapeDtypeStruct((rows, LANES), jnp.float32)] * count

    def params(mebibytes):
        return pltpu.CompilerParams(vmem_limit_bytes=mebibytes * 1024 * 1024)

    given = (window, lookback, queries, key_rows, value_rows, cotangent)

    def pack(some, name):
        return pl.pallas_call(
            lambda *refs: pack_kernel(some, parts, *refs),
            out_shape=blocks(len(some), 4 * patches_here + INFO),
            in_specs=[anywhere] * 6,
            out_specs=[vmem] * len(some),
            scratch_shapes=[held] * 4 + smem + [dma((10,))],
            compiler_params=params(56),
            name=name,
        )(*given)

    packed = pack(order[1 : 1 + FIRST], "pack_heads")
    packed = *packed, *pack(order[1 + FIRST :], "pack_rest")
    done = pl.pallas_call(
        lambda *refs: head_kernel(order, back, groups, parts, *refs),
        out_shape=blocks(H, 4 * patches_here),
        in_specs=[anywhere] * 6 + [vmem] * (H - 1),
        out_specs=[vmem] * H,
        scratch_shapes=[pltpu.VMEM((2, patches_here, LANES), jnp.float32)] * 4
        + [pltpu.VMEM((4 * patches_here, LANES), jnp.float32)]
        + smem
        + [pltpu.VMEM((groups, INFO, LANES), jnp.float32), dma((6,))]
        + [across] * 10
        + [
            pltpu.VMEM((frames, 8, patches), jnp.float32),
            pltpu.VMEM((LANES, patches), jnp.bfloat16),
            pltpu.VMEM((patches, LANES), jnp.bfloat16),
        ],
        compiler_params=params(24),
        name="one_head",
    )(*given, *exchange(packed, order[1:], parts))
    return pl.pallas_call(
        lambda *refs: unpack_kernel(back, groups, parts, *refs),
        out_shape=[jax.ShapeDtypeStruct(queries.shape, jnp.float32)] * 4,
        in_specs=[vmem] * H,
        out_specs=[anywhere] * 4,
        scratch_shapes=[
            pltpu.VMEM((H // 2, 4, 2, patches_here, LANES), jnp.float32),
            dma((2 * H,)),
        ],
        compiler_params=params(40),
        name="unpack_heads",
    )(done[0], *exchange(done[1:], back[1:], parts))


def shards(queries, key_rows, value_rows, cotangent, lookback, window):
    frames_here, patches_here, model_width = queries.shape
    fits = (
        lax.axis_size("frame") * lax.axis_size("patch") == H
        and lax.axis_size("patch") == 4
        and frames_here == 2
        and patches_here == SIZE
        and model_width == H * SIZE
    )
    form = shards_by_head if fits else shards_general
    return tuple(form(queries, key_rows, value_rows, cotangent, lookback, window))


def solution(mesh):
    rows = P(("traj", "frame"), "patch", None)
    return jax.shard_map(
        shards,
        mesh=mesh,
        in_specs=(rows, rows, rows, rows, P(("traj", "frame")), P(("traj", "patch"), None)),
        out_specs=(rows,) * 4,
        check_vma=False,
    )
```

```python
import math

import jax
import jax.numpy as jnp
from jax import lax
from jax.experimental import pallas as pl
from jax.experimental.pallas import tpu as pltpu
from jax.sharding import PartitionSpec as P

H = 16
BLK = 16
LOOK = 6
REACH = 6


def shifted(x, axis, by):
    count = lax.axis_size(axis)
    pairs = [(i, i + by) for i in range(count) if 0 <= i + by < count]
    return lax.ppermute(x, axis, pairs)


def passed_along(block, axis, distance):
    devices = range(lax.axis_size(axis))
    route = [((i - distance) % len(devices), i) for i in devices]
    return lax.ppermute(block, axis, route)


def split_heads(tensor, size_head):
    return tensor.reshape(tensor.shape[0], tensor.shape[1], H, size_head)


def shards_general(queries, key_rows, value_rows, cotangent, lookback, window):
    frames_here, patches_here, model_width = queries.shape
    size_head = model_width // H
    score_scale = 1.0 / math.sqrt(size_head)
    highest = lax.Precision.HIGHEST
    frame_index = lax.axis_index("frame")
    cycle_depth = (LOOK + frames_here - 2) // frames_here
    earlier = []
    carried = (key_rows, value_rows)
    for distance in range(cycle_depth):
        carried = shifted((carried[0], carried[1]), "frame", 1)
        earlier.append(carried)
    bank_keys = jnp.concatenate(
        [earlier[cycle_depth - 1 - number][0] for number in range(cycle_depth)] + [key_rows], axis=0
    )
    bank_values = jnp.concatenate(
        [earlier[cycle_depth - 1 - number][1] for number in range(cycle_depth)] + [value_rows],
        axis=0,
    )
    bank_frames = bank_keys.shape[0]
    q_heads = split_heads(queries, size_head)
    key_heads = split_heads(bank_keys, size_head)
    value_heads = split_heads(bank_values, size_head)
    query_frame = frame_index * frames_here + jnp.arange(frames_here, dtype=jnp.int32)
    key_frame = (frame_index - cycle_depth) * frames_here + jnp.arange(bank_frames, dtype=jnp.int32)
    offset = query_frame[:, None] - key_frame[None, :]
    visible = (offset >= 0) & (offset < lookback[:, None]) & (key_frame[None, :] >= 0)
    scores = jnp.einsum("fphe,jphe->phfj", q_heads, key_heads, precision=highest) * score_scale
    scores = jnp.where(visible, scores, -jnp.inf)
    weights = jax.nn.softmax(scores, axis=-1)
    temporal = jnp.einsum("phfj,jphe->fphe", weights, value_heads, precision=highest).reshape(
        frames_here, patches_here, model_width
    )
    patch_count = lax.axis_size("patch")
    patch_index = lax.axis_index("patch")
    blocks_here = patches_here // BLK
    reach_devices = -(-REACH // blocks_here)
    offsets = []
    for stride in range(-reach_devices, reach_devices + 1):
        if all(((stride - earlier_step) % patch_count != 0 for earlier_step in offsets)):
            offsets.append(stride)
    entries = []
    running_base = 0
    for stride in offsets:
        count_here = blocks_here if stride != 0 and abs(stride) == reach_devices else blocks_here
        first_block = 0 if stride >= 0 else blocks_here - count_here
        entries.append((stride, first_block, count_here, running_base))
        running_base = running_base + count_here
    count_slots = running_base
    near_banks = []
    for stride, first_block, count_here, base_slot in entries:
        rows_from = first_block * BLK
        rows_to = (first_block + count_here) * BLK
        piece = (key_rows, temporal)
        if stride == 0:
            near_banks.append(piece)
        else:
            near_banks.append(passed_along((piece[0], piece[1]), "patch", -stride))
    near_keys = jnp.concatenate([entry[0] for entry in near_banks], axis=1)
    near_values = jnp.concatenate([entry[1] for entry in near_banks], axis=1)
    owner_device = window // blocks_here
    relative = (owner_device - patch_index) % patch_count
    base_of = jnp.zeros(window.shape, jnp.int32)
    first_of = jnp.zeros(window.shape, jnp.int32)
    for stride, first_block, count_here, base_slot in entries:
        matches = relative == stride % patch_count
        base_of = jnp.where(matches, base_slot, base_of)
        first_of = jnp.where(matches, first_block, first_of)
    slot_index = base_of + window % blocks_here - first_of
    window_count = window.shape[1]
    key_blocks = near_keys.reshape(frames_here, count_slots, BLK, model_width)
    value_blocks = near_values.reshape(frames_here, count_slots, BLK, model_width)

    def frame_step(frame_items):
        query_part, key_part, value_part, grad_part = frame_items
        key_win = key_part[slot_index].reshape(blocks_here, window_count * BLK, H, size_head)
        value_win = value_part[slot_index].reshape(blocks_here, window_count * BLK, H, size_head)
        query_win = query_part.reshape(blocks_here, BLK, H, size_head)
        grad_win = grad_part.reshape(blocks_here, BLK, H, size_head)
        logits = jnp.einsum("bxhe,byhe->bhxy", query_win, key_win, precision=highest) * score_scale
        attention = jax.nn.softmax(logits, axis=-1)
        mixed_rows = jnp.einsum("bhxy,byhe->bxhe", attention, value_win, precision=highest)
        grad_attention = jnp.einsum("bxhe,byhe->bhxy", grad_win, value_win, precision=highest)
        grad_logits = attention * (
            grad_attention - jnp.sum(attention * grad_attention, axis=-1, keepdims=True)
        )
        grad_query = (
            jnp.einsum("bhxy,byhe->bxhe", grad_logits, key_win, precision=highest) * score_scale
        )
        grad_key = (
            jnp.einsum("bhxy,bxhe->byhe", grad_logits, query_win, precision=highest) * score_scale
        )
        grad_value = jnp.einsum("bhxy,bxhe->byhe", attention, grad_win, precision=highest)
        block_shape = (blocks_here, window_count, BLK, model_width)
        key_back = (
            jnp.zeros((count_slots, BLK, model_width), jnp.float32)
            .at[slot_index]
            .add(grad_key.reshape(block_shape))
        )
        value_back = (
            jnp.zeros((count_slots, BLK, model_width), jnp.float32)
            .at[slot_index]
            .add(grad_value.reshape(block_shape))
        )
        return (
            mixed_rows.reshape(patches_here, model_width),
            grad_query.reshape(patches_here, model_width),
            key_back,
            value_back,
        )

    mixed, grad_query_space, key_back, value_back = lax.map(
        frame_step, (queries, key_blocks, value_blocks, cotangent)
    )
    key_back = key_back.reshape(frames_here, count_slots * BLK, model_width)
    value_back = value_back.reshape(frames_here, count_slots * BLK, model_width)
    grad_key_space = jnp.zeros(queries.shape, jnp.float32)
    grad_temporal = jnp.zeros(queries.shape, jnp.float32)
    for stride, first_block, count_here, base_slot in entries:
        slot_from = base_slot * BLK
        slot_to = (base_slot + count_here) * BLK
        returned = (key_back[:, slot_from:slot_to], value_back[:, slot_from:slot_to])
        if stride != 0:
            returned = passed_along((returned[0], returned[1]), "patch", stride)
        rows_from = first_block * BLK
        rows_to = (first_block + count_here) * BLK
        grad_key_space = grad_key_space.at[:, rows_from:rows_to].add(returned[0])
        grad_temporal = grad_temporal.at[:, rows_from:rows_to].add(returned[1])
    grad_heads = split_heads(grad_temporal, size_head)
    grad_weights = jnp.einsum("fphe,jphe->phfj", grad_heads, value_heads, precision=highest)
    grad_scores = weights * (grad_weights - jnp.sum(weights * grad_weights, axis=-1, keepdims=True))
    grad_query_time = (
        jnp.einsum("phfj,jphe->fphe", grad_scores, key_heads, precision=highest) * score_scale
    )
    key_terms = (
        jnp.einsum("phfj,fphe->jphe", grad_scores, q_heads, precision=highest) * score_scale
    ).reshape(cycle_depth + 1, frames_here, patches_here, model_width)
    value_terms = jnp.einsum("phfj,fphe->jphe", weights, grad_heads, precision=highest).reshape(
        cycle_depth + 1, frames_here, patches_here, model_width
    )
    carried = (key_terms[0], value_terms[0])
    for distance in range(1, cycle_depth + 1):
        carried = shifted((carried[0], carried[1]), "frame", -1)
        carried = (carried[0] + key_terms[distance], carried[1] + value_terms[distance])
    grad_key_time, grad_value_time = carried
    grad_queries = grad_query_space + grad_query_time.reshape(
        frames_here, patches_here, model_width
    )
    grad_keys = grad_key_space + grad_key_time
    return (mixed, grad_queries, grad_keys, grad_value_time)


LANES = 128
SIZE = LANES // 2
INFO = 8
OUTWARD = (
    (0, 0), (0, 3), (3, 0), (2, 2), (2, 1), (1, 0), (1, 2), (1, 1),
    (1, 3), (2, 0), (3, 2), (0, 1), (0, 2), (3, 1), (2, 3), (3, 3),
)
HOMEWARD = (
    (0, 0), (0, 3), (3, 0), (2, 2), (2, 1), (1, 0), (1, 2), (1, 1),
    (1, 3), (2, 0), (3, 2), (0, 1), (0, 2), (3, 1), (2, 3), (3, 3),
)
FIRST = 5
HIDDEN = -1e30
NN = ((1,), (0,))
NT = ((1,), (1,))


def interleave(first, second):
    axis = first.ndim - 1
    low = lax.broadcasted_iota(jnp.int32, first.shape, axis) < SIZE
    return (
        jnp.where(low, first, pltpu.roll(second, SIZE, axis)),
        jnp.where(low, pltpu.roll(first, SIZE, axis), second),
    )


def dot(a, b, dims):
    return lax.dot_general(a, b, (dims, ((), ())), preferred_element_type=jnp.float32)


def split(x):
    high = x.astype(jnp.bfloat16)
    return high, (x - high.astype(jnp.float32)).astype(jnp.bfloat16)


def stacked(x, times):
    high, low = split(x)
    return jnp.concatenate([high] * times + [low] * times, axis=0)


def heads_dot(x, high, low, dims):
    both = stacked(x, 1)
    out = dot(both, high, dims)
    return out[:SIZE] + (out[SIZE:] + dot(both[:SIZE], low, dims))


def place(partner, patch_count):
    frame = lax.bitwise_xor(lax.axis_index("frame"), partner[0])
    return frame * patch_count + lax.bitwise_xor(lax.axis_index("patch"), partner[1])


def columns_of(head):
    return pl.ds(pl.multiple_of(head // 2 * LANES, LANES), LANES)


def low_lanes(rows):
    return lax.broadcasted_iota(jnp.int32, (rows, LANES), 1) < SIZE


def side_by_side(ref, head, cols):
    odd = head % 2
    kept, moved = ref[odd, :, cols], ref[1 - odd, :, cols]
    low = low_lanes(kept.shape[0]).astype(jnp.int32)
    return jnp.where(low != odd, kept, pltpu.roll(moved, SIZE, 1))


def whole_numbers(window, lookback, rows):
    row = lax.broadcasted_iota(jnp.int32, (INFO, LANES), 0)
    lane = lax.broadcasted_iota(jnp.int32, (INFO, LANES), 1)
    info = jnp.zeros((INFO, LANES), jnp.int32)
    for block in range(rows // BLK):
        for column in range(window.shape[1]):
            at = block * BLK + (column // INFO) * SIZE
            here = (row == column % INFO) & (lane >= at) & (lane < at + BLK)
            info = jnp.where(here, window[block, column], info)
    for frame in range(2):
        here = (row == INFO - 2 + frame) & (lane >= SIZE)
        info = jnp.where(here, lookback[frame], info)
    return info.astype(jnp.float32)


def fetch(moves, sems):
    copies = [pltpu.make_async_copy(a, b, sems.at[n]) for n, (a, b) in enumerate(moves)]
    for copy in copies:
        copy.start()
    return copies


def pack_kernel(order, parts, window, lookback, *refs):
    arrays, out_refs, refs = refs[:4], refs[4 : 4 + len(order)], refs[4 + len(order) :]
    held, window_ref, lookback_ref, sems = refs[:4], *refs[4:]
    moves = [(window, window_ref), (lookback, lookback_ref)]
    moves += [(a.at[frame], b.at[frame]) for a, b in zip(arrays, held) for frame in range(2)]
    copies = fetch(moves, sems)
    copies[0].wait()
    copies[1].wait()
    rows = held[0].shape[1]
    info = whole_numbers(window_ref, lookback_ref, rows)
    for ref in out_refs:
        ref[4 * rows :] = info
    for number, ref in enumerate(held):
        copies[2 + 2 * number].wait()
        copies[3 + 2 * number].wait()
        for partner, out_ref in zip(order, out_refs):
            head = place(partner, parts)
            out_ref[rows_of(number, rows)] = side_by_side(ref, head, columns_of(head))


def unpack_kernel(order, groups, parts, *refs):
    in_refs, out_refs, held, sems = refs[:H], refs[H : H + 4], refs[H + 4], refs[H + 5]
    rows = held.shape[3]
    pairs = [(frame, patch) for frame in range(groups) for patch in range(0, parts, 2)]
    copies = []
    for n, (frame, patch) in enumerate(pairs):
        head = place((frame, patch), parts)
        odd = jnp.full((rows, LANES), head % 2, jnp.int32) == 1
        for m, out_ref in enumerate(out_refs):
            at = rows_of(m, rows)
            here = in_refs[order.index((frame, patch))][at]
            there = in_refs[order.index((frame, patch + 1))][at]
            held[n, m, 0], held[n, m, 1] = interleave(
                jnp.where(odd, there, here), jnp.where(odd, here, there)
            )
            copies.append(
                pltpu.make_async_copy(
                    held.at[n, m], out_ref.at[:, :, columns_of(head)], sems.at[4 * n + m]
                )
            )
            copies[-1].start()
    for copy in copies:
        copy.wait()


def visible_keys(frame):
    return range(max(0, frame - LOOK + 1), frame + 1)


def rows_of(index, count):
    return slice(index * count, (index + 1) * count)


def head_kernel(order, back, groups, parts, window, lookback, *refs):
    arrays, in_refs, out_refs = refs[:4], refs[4 : 3 + H], refs[3 + H : 3 + 2 * H]
    held, own_ref, window_ref, lookback_ref, lookbacks, sems = refs[3 + 2 * H : 12 + 2 * H][:4], *refs[
        7 + 2 * H : 12 + 2 * H
    ]
    qt, kt, vt, ct, tt, mt, gt, gq, gk, gv, wts, bias, blocks = refs[12 + 2 * H :]
    rows = own_ref.shape[0] // 4
    frames, _, patches = wts.shape
    scale = 1.0 / math.sqrt(SIZE)

    head = place((0, 0), parts)
    moves = [(window, window_ref), (lookback, lookback_ref)]
    moves += [(a.at[:, :, columns_of(head)], b) for a, b in zip(arrays, held)]
    copies = fetch(moves, sems)

    def natural(number, group):
        at = rows_of(number, rows)
        found = [in_refs[order.index((group, part)) - 1][at] if group or part else own_ref[at] for part in range(parts)]
        return jnp.concatenate(found, axis=0)

    def tile(group, part):
        return in_refs[order.index((group, part)) - 1][4 * rows :] if group or part else info

    def pair_rows(group):
        at = lax.bitwise_xor(lax.axis_index("frame"), group) * LANES
        return pl.ds(pl.multiple_of(at, LANES), LANES)

    def turn(group):
        at = pair_rows(group)
        qt[at] = natural(0, group).T * scale
        kt[at] = natural(1, group).T
        vt[at] = natural(2, group).T
        ct[at] = natural(3, group).T
        lookbacks[lax.bitwise_xor(lax.axis_index("frame"), group)] = tile(group, 0)

    for group in range(1, groups):
        turn(group)
    for copy in copies:
        copy.wait()
    for number, ref in enumerate(held):
        own_ref[rows_of(number, rows)] = side_by_side(ref, head, slice(None))
    info = whole_numbers(window_ref, lookback_ref, rows)
    turn(0)

    sides = [interleave(tile(0, part), tile(0, part + 1)) for part in range(0, parts, 2)]
    first = jnp.concatenate([side[0] for side in sides], axis=1)
    last = jnp.concatenate([side[1] for side in sides], axis=1)
    count = rows // BLK
    block = lax.broadcasted_iota(jnp.int32, (parts * count, patches), 0)
    block = lax.bitwise_xor(block // count, lax.axis_index("patch")) * count + block % count
    block = block.astype(jnp.float32)
    seen = block == first[0:1]
    for column in range(1, window.shape[1]):
        of = first if column < INFO else last
        seen = seen | (block == of[column % INFO : column % INFO + 1])
    mask = jnp.where(seen, 0.0, HIDDEN).astype(jnp.bfloat16)
    spare = jnp.zeros((LANES - parts * count, patches), jnp.bfloat16)
    bias[...] = jnp.concatenate([mask, spare], axis=0)
    key_block = lax.broadcasted_iota(jnp.int32, (patches, LANES), 0) // BLK
    lane = lax.broadcasted_iota(jnp.int32, (patches, LANES), 1)
    blocks[...] = jnp.where(key_block == lane, 1.0, 0.0).astype(jnp.bfloat16)

    def look_back(frame):
        _, given = interleave(lookbacks[frame // 2], lookbacks[frame // 2])
        at = INFO - 2 + frame % 2
        seen_frames = given[at : at + 1]
        for chunk in range(patches // LANES):
            cols = rows_of(chunk, LANES)
            query = qt[rows_of(frame, SIZE), cols]
            keys = visible_keys(frame)
            scores = []
            for key in keys:
                score = jnp.sum(query * kt[rows_of(key, SIZE), cols], axis=0, keepdims=True)
                scores.append(jnp.where(seen_frames > float(frame - key), score, -jnp.inf))
            top = scores[0]
            for score in scores[1:]:
                top = jnp.maximum(top, score)
            exps = [jnp.exp(score - top) for score in scores]
            total = exps[0]
            for term in exps[1:]:
                total = total + term
            value = jnp.zeros((SIZE, LANES), jnp.float32)
            for key, term in zip(keys, exps):
                weight = term / total
                wts[frame, frame - key : frame - key + 1, cols] = weight
                value = value + weight * vt[rows_of(key, SIZE), cols]
            tt[rows_of(frame, SIZE), cols] = value

    state = {}

    def products(frame):
        mine = rows_of(frame, SIZE)
        if frame % 2 == 0:
            at = rows_of(frame // 2, LANES)
            keys = kt[at].T
            high = keys.astype(jnp.bfloat16).astype(jnp.float32)
            low = keys - high
            mid = low.astype(jnp.bfloat16).astype(jnp.float32)
            upper = [x.astype(jnp.bfloat16) for x in interleave(high, mid)]
            lower = [x.astype(jnp.bfloat16) for x in interleave(high, low - mid)]
            value = tt[at].T
            high = value.astype(jnp.bfloat16).astype(jnp.float32)
            values = [x.astype(jnp.bfloat16) for x in interleave(high, value - high)]
            state["pair"] = list(zip(upper, lower, values))
        upper, lower, value = state["pair"][frame % 2]
        query = qt[mine]
        high, mid = split(query)
        low = query - high.astype(jnp.float32) - mid.astype(jnp.float32)
        low = low.astype(jnp.bfloat16)
        logits = dot(
            jnp.concatenate([upper] * 2, axis=1),
            jnp.concatenate([high, high, mid, mid], axis=0),
            NN,
        )
        logits = logits + dot(
            jnp.concatenate([lower, blocks[...]], axis=1),
            jnp.concatenate([low, high, bias[...]], axis=0),
            NN,
        )
        grad_weights = dot(jnp.concatenate([value] * 2, axis=1), stacked(ct[mine], 2), NN)
        state[frame] = logits, grad_weights

    def weigh(frame):
        logits, grad_weights = state[frame]
        top = jnp.max(logits, axis=0, keepdims=True)
        exps = jnp.exp(logits - top)
        share = 1.0 / jnp.sum(exps, axis=0, keepdims=True)
        state[frame] = exps, *split(exps), share, grad_weights

    def mix(frame):
        mine = rows_of(frame, SIZE)
        exps, high, low, share, grad_weights = state[frame]
        mt[mine] = heads_dot(tt[mine], high, low, NN) * share
        gt[mine] = heads_dot(ct[mine] * share, high, low, NT)

    def differ(frame):
        mine = rows_of(frame, SIZE)
        exps, _, _, share, grad_weights = state[frame]
        delta = jnp.sum(ct[mine] * mt[mine], axis=0, keepdims=True)
        state[frame] = *split(exps * (grad_weights - delta)), share

    def finish(frame):
        mine = rows_of(frame, SIZE)
        high, low, share = state.pop(frame)
        gq[mine] = heads_dot(kt[mine], high, low, NN) * share
        gk[mine] = heads_dot(qt[mine] * share, high, low, NT)

    def hand_back(frame):
        mine = rows_of(frame, SIZE)
        for chunk in range(patches // LANES):
            cols = rows_of(chunk, LANES)
            query, grad = qt[mine, cols], gt[mine, cols]
            weights, terms = [], []
            inner = jnp.zeros((1, LANES), jnp.float32)
            for key in visible_keys(frame):
                weight = wts[frame, frame - key : frame - key + 1, cols]
                term = jnp.sum(grad * vt[rows_of(key, SIZE), cols], axis=0, keepdims=True)
                inner = inner + weight * term
                weights.append(weight)
                terms.append(term)
            grad_query = gq[mine, cols]
            for key, weight, term in zip(visible_keys(frame), weights, terms):
                of = rows_of(key, SIZE)
                score = weight * (term - inner)
                grad_query = grad_query + score * kt[of, cols]
                gk[of, cols] = gk[of, cols] + score * query
                if key == frame:
                    gv[of, cols] = weight * grad
                else:
                    gv[of, cols] = gv[of, cols] + weight * grad
            gq[mine, cols] = grad_query * scale

    for step in range(frames + 5):
        for late, does in (
            (0, look_back),
            (2, products),
            (3, weigh),
            (4, differ),
            (3, mix),
            (4, finish),
            (5, hand_back),
        ):
            if 0 <= step - late < frames:
                does(step - late)

    for group in range(groups):
        for number, ref in enumerate((mt, gq, gk, gv)):
            turned = ref[pair_rows(group)].T
            for part in range(parts):
                at = rows_of(number, rows)
                out_refs[back.index((group, part))][at] = turned[rows_of(part, rows)]


def exchange(blocks, order, patch_count):
    return [
        lax.ppermute(
            block,
            ("frame", "patch"),
            [
                (i * patch_count + j, (i ^ frame) * patch_count + (j ^ patch))
                for i in range(H // patch_count)
                for j in range(patch_count)
            ],
        )
        for block, (frame, patch) in zip(blocks, order)
    ]


def shards_by_head(queries, key_rows, value_rows, cotangent, lookback, window):
    frames_here, patches_here, model_width = queries.shape
    groups, parts = lax.axis_size("frame"), lax.axis_size("patch")
    frames, patches = frames_here * groups, patches_here * parts
    order = OUTWARD
    back = HOMEWARD
    vmem = pl.BlockSpec(memory_space=pltpu.VMEM)
    anywhere = pl.BlockSpec(memory_space=pl.ANY)
    dma = pltpu.SemaphoreType.DMA
    held = pltpu.VMEM(queries.shape, jnp.float32)
    smem = [pltpu.SMEM(window.shape, jnp.int32), pltpu.SMEM(lookback.shape, jnp.int32)]
    across = pltpu.VMEM((frames * SIZE, patches), jnp.float32)

    def blocks(count, rows):
        return [jax.ShapeDtypeStruct((rows, LANES), jnp.float32)] * count

    def params(mebibytes):
        return pltpu.CompilerParams(vmem_limit_bytes=mebibytes * 1024 * 1024)

    given = (window, lookback, queries, key_rows, value_rows, cotangent)

    def pack(some, name):
        return pl.pallas_call(
            lambda *refs: pack_kernel(some, parts, *refs),
            out_shape=blocks(len(some), 4 * patches_here + INFO),
            in_specs=[anywhere] * 6,
            out_specs=[vmem] * len(some),
            scratch_shapes=[held] * 4 + smem + [dma((10,))],
            compiler_params=params(56),
            name=name,
        )(*given)

    packed = pack(order[1 : 1 + FIRST], "pack_heads")
    packed = *packed, *pack(order[1 + FIRST :], "pack_rest")
    done = pl.pallas_call(
        lambda *refs: head_kernel(order, back, groups, parts, *refs),
        out_shape=blocks(H, 4 * patches_here),
        in_specs=[anywhere] * 6 + [vmem] * (H - 1),
        out_specs=[vmem] * H,
        scratch_shapes=[pltpu.VMEM((2, patches_here, LANES), jnp.float32)] * 4
        + [pltpu.VMEM((4 * patches_here, LANES), jnp.float32)]
        + smem
        + [pltpu.VMEM((groups, INFO, LANES), jnp.float32), dma((6,))]
        + [across] * 10
        + [
            pltpu.VMEM((frames, 8, patches), jnp.float32),
            pltpu.VMEM((LANES, patches), jnp.bfloat16),
            pltpu.VMEM((patches, LANES), jnp.bfloat16),
        ],
        compiler_params=params(24),
        name="one_head",
    )(*given, *exchange(packed, order[1:], parts))
    return pl.pallas_call(
        lambda *refs: unpack_kernel(back, groups, parts, *refs),
        out_shape=[jax.ShapeDtypeStruct(queries.shape, jnp.float32)] * 4,
        in_specs=[vmem] * H,
        out_specs=[anywhere] * 4,
        scratch_shapes=[
            pltpu.VMEM((H // 2, 4, 2, patches_here, LANES), jnp.float32),
            dma((2 * H,)),
        ],
        compiler_params=params(40),
        name="unpack_heads",
    )(done[0], *exchange(done[1:], back[1:], parts))


def shards(queries, key_rows, value_rows, cotangent, lookback, window):
    frames_here, patches_here, model_width = queries.shape
    fits = (
        lax.axis_size("frame") * lax.axis_size("patch") == H
        and lax.axis_size("patch") == 4
        and frames_here == 2
        and patches_here == SIZE
        and model_width == H * SIZE
    )
    form = shards_by_head if fits else shards_general
    return tuple(form(queries, key_rows, value_rows, cotangent, lookback, window))


def solution(mesh):
    rows = P(("traj", "frame"), "patch", None)
    return jax.shard_map(
        shards,
        mesh=mesh,
        in_specs=(rows, rows, rows, rows, P(("traj", "frame")), P(("traj", "patch"), None)),
        out_specs=(rows,) * 4,
        check_vma=False,
    )
```
